512 devices in a mesh: gx: 4 (over y_hi, core), gy: 4 (over x), gz: 32 (over y_lo, z).
Axes of the slice: x: 4, y: 4 (y_hi: 2, y_lo: 2; y = y_hi * 2 + y_lo), z: 16, core: 2. Of those that a mesh axis runs over, the one named last changes fastest.
Arguments:
- features: bfloat16 [4, 4, 32, 64, 3200], P('gx', 'gy', 'gz'), may hold values from -6 to 6
- positions: float32 [4, 4, 32, 3, 64], P('gx', 'gy', 'gz'), as said below
- neighbours: int32 [4, 4, 32, 64, 32], P('gx', 'gy', 'gz'), may hold values from 0 to 575, as said below
- counts: int32 [4, 4, 32, 64], P('gx', 'gy', 'gz'), may hold values from 8 to 32, as said below
- cell_atoms: int32 [4, 4, 32, 64], P('gx', 'gy', 'gz'), may hold values from 0 to 63, as said below
- rbf_weight: bfloat16 [512, 128], replicated, may hold values from -3 to 3
- radial_weight: bfloat16 [128, 640], replicated, may hold values from -0.5 to 0.5
- mix_weight: bfloat16 [5, 128, 128], replicated, may hold values from -0.5 to 0.5
- out_weight: bfloat16 [5, 128, 128], replicated, may hold values from -1 to 1
- energy_weight: float32 [128], replicated, may hold values from -0.5 to 0.5
- norm_weight: float32 [4, 128], replicated, may hold values from -0.5 to 0.5
Outputs:
- new_features: bfloat16 [4, 4, 32, 64, 3200], P('gx', 'gy', 'gz')
- energies: float32 [4, 4, 32, 64], P('gx', 'gy', 'gz')
- forces: float32 [4, 4, 32, 3, 64], P('gx', 'gy', 'gz')
The draws below stay inside these ranges and needn't reach their ends.
Inputs may be any that keep to these rules, and one draw needn't show every extreme that they name: `positions`: the atom cell_atoms[q] of cell slot q = 8 c + r lies within 0.2 of the lattice site (2 cx + rx + 0.5, 2 cy + ry + 0.5, 2 cz + rz + 0.5) of its box. `neighbours`: the first 16 slots of atom i name other atoms of its domain (rows 0 to 63, never i); the rest name rows 64 + 8 e + r of extended cells e = ((ex 4 + ey) (4) + ez) that touch atom i's cell and lie outside the domain. `counts`: atom 0 of every domain has all 32 slots live. `cell_atoms`: A permutation of the domain's atoms.
All inputs are finite; a program needn't handle non-finite values.
Results may differ from the reference program's by a relative error of at most 0.012.
Values may be sent and summed in bfloat16 or wider, within the bound.
A program may use at most 64 MiB of HBM per device.

```python
import math
from functools import partial
import jax
import jax.numpy as jnp
import numpy as np
from jax import lax

C = 128
LMAX = 4
FEAT = 3200
RBF = 512
HID = 128
NB = 32
ZCELLS = 2
ATOM_DEV = 64
N_GX = 4
N_GY = 4
N_GZ = 32


def cell_order(key):
    atom_total = 32 * ZCELLS
    scores = jax.random.randint(jax.random.fold_in(key, 51), (N_GX, N_GY, N_GZ, atom_total), 0, 1 << 20) * atom_total + jnp.arange(atom_total, dtype=jnp.int32)
    return jnp.argsort(scores, axis=-1).astype(jnp.int32)


def slot_coords(slot_of):
    cell = slot_of // 8
    within = slot_of % 8
    cell_x = cell // (2 * ZCELLS)
    cell_y = cell // ZCELLS % 2
    cell_z = cell % ZCELLS
    return (cell_x, cell_y, cell_z, within)


def draw_cell_atoms(key, part):
    return cell_order(key)


def draw_positions(key, part):
    atom_total = 32 * ZCELLS
    slot_of = jnp.argsort(cell_order(key), axis=-1).astype(jnp.int32)
    cell_x, cell_y, cell_z, within = slot_coords(slot_of)
    lattice = jnp.stack([2 * cell_x + within // 4, 2 * cell_y + within // 2 % 2, 2 * cell_z + within % 2], axis=3).astype(jnp.float32) + 0.5
    shape = (N_GX, N_GY, N_GZ, 3, atom_total)
    noise_key = jax.random.fold_in(key, 11)
    jitter = jnp.clip(0.07 * jax.random.normal(noise_key, shape, jnp.float32), -0.2, 0.2)
    return lattice + jitter


def draw_neighbours(key, part):
    atom_total = 32 * ZCELLS
    half_slots = NB // 2
    shape = (N_GX, N_GY, N_GZ, atom_total)
    own_pick = jax.random.randint(jax.random.fold_in(key, 21), shape + (half_slots,), 0, atom_total - 1)
    own_rows = (jnp.arange(atom_total, dtype=jnp.int32)[:, None] + 1 + own_pick) % atom_total
    slot_of = jnp.argsort(cell_order(key), axis=-1).astype(jnp.int32)
    cell_x, cell_y, cell_z, within = slot_coords(slot_of)
    cell_x = cell_x[..., None]
    cell_y = cell_y[..., None]
    cell_z = cell_z[..., None]
    ghost_shape = shape + (NB - half_slots,)
    axis_pick = jax.random.randint(jax.random.fold_in(key, 22), ghost_shape, 0, 3)
    step_x = jax.random.randint(jax.random.fold_in(key, 23), ghost_shape, -1, 2)
    step_y = jax.random.randint(jax.random.fold_in(key, 24), ghost_shape, -1, 2)
    step_z = jax.random.randint(jax.random.fold_in(key, 25), ghost_shape, -1, 2)
    sign_pick = jax.random.randint(jax.random.fold_in(key, 26), ghost_shape, 0, 2) * 2 - 1
    row_pick = jax.random.randint(jax.random.fold_in(key, 27), ghost_shape, 0, 8)
    out_x = jnp.where(cell_x == 0, -1, 1)
    out_y = jnp.where(cell_y == 0, -1, 1)
    low_z = cell_z == 0
    high_z = cell_z == ZCELLS - 1
    out_z = jnp.where(jnp.logical_and(low_z, high_z), sign_pick, jnp.where(low_z, -1, 1))
    edge_z = jnp.logical_or(low_z, high_z)
    axis_used = jnp.where(jnp.logical_and(axis_pick == 2, jnp.logical_not(edge_z)), 0, axis_pick)
    move_x = jnp.where(axis_used == 0, out_x, step_x)
    move_y = jnp.where(axis_used == 1, out_y, step_y)
    move_z = jnp.where(axis_used == 2, out_z, step_z)
    extended = ((cell_x + 1 + move_x) * 4 + (cell_y + 1 + move_y)) * (ZCELLS + 2) + (cell_z + 1 + move_z)
    ghost_rows = atom_total + extended * 8 + row_pick
    return jnp.concatenate([own_rows, ghost_rows], axis=-1).astype(jnp.int32)


def draw_counts(key, part):
    atom_total = 32 * ZCELLS
    drawn = jax.random.randint(jax.random.fold_in(key, 31), (N_GX, N_GY, N_GZ, atom_total), NB // 4, NB + 1)
    return drawn.at[:, :, :, 0].set(NB).astype(jnp.int32)


def level_of(key, dims, pieces, low, high):
    loudness = 1.0
    for position, blocks in pieces:
        steps = jax.random.uniform(jax.random.fold_in(jax.random.fold_in(key, 6), position), (blocks,), jnp.float32, low / len(pieces), high / len(pieces))
        loudness = loudness * jnp.repeat(jnp.exp(steps), dims[position] // blocks).reshape((-1,) + (1,) * (len(dims) - 1 - position))
    return loudness


def noise(rng, shape, deviation, limit, pieces=(), kind=jnp.bfloat16):
    values = jax.random.normal(rng, shape, jnp.float32) * deviation
    if len(pieces) > 0:
        values = level_of(rng, shape, pieces, -0.22, 0.18) * values
    return jnp.clip(values, min=-limit, max=limit).astype(kind)


def setup_inputs(seed: int = 0) -> dict:
    streams_of = jax.random.split(jax.random.key(seed), 12)
    features = noise(streams_of[0], (N_GX, N_GY, N_GZ, ATOM_DEV, FEAT), 1.0, 6.0, ((0, 4), (1, 4), (2, 32)))
    positions = draw_positions(jax.random.fold_in(streams_of[11], 71), 0)
    neighbours = draw_neighbours(jax.random.fold_in(streams_of[11], 71), 0)
    counts = draw_counts(jax.random.fold_in(streams_of[11], 71), 0)
    cell_atoms = draw_cell_atoms(jax.random.fold_in(streams_of[11], 71), 0)
    rbf_weight = noise(streams_of[5], (RBF, HID), 4 ** -0.5, 3.0)
    radial_weight = noise(streams_of[6], (HID, (LMAX + 1) * C), HID ** -0.5, 0.5)
    mix_weight = noise(streams_of[7], (LMAX + 1, C, C), C ** -0.5, 0.5)
    out_weight = noise(streams_of[8], (LMAX + 1, C, C), (C // 4) ** -0.5, 1.0)
    energy_weight = noise(streams_of[9], (C,), C ** -0.5, 0.5, (), jnp.float32)
    norm_weight = noise(streams_of[10], (LMAX, C), C ** -0.5, 0.5, (), jnp.float32)
    return dict(features=features, positions=positions, neighbours=neighbours, counts=counts, cell_atoms=cell_atoms, rbf_weight=rbf_weight, radial_weight=radial_weight, mix_weight=mix_weight, out_weight=out_weight, energy_weight=energy_weight, norm_weight=norm_weight)


def degree_of(coeff_total):
    top_degree = int(math.isqrt(coeff_total)) - 1
    return np.array([degree for degree in range(top_degree + 1) for _ in range(2 * degree + 1)], dtype=np.int32)

def product(pattern, first_op, second_op):
    return jnp.einsum(pattern, first_op.astype(jnp.float32), second_op.astype(jnp.float32), preferred_element_type=jnp.float32)

def image_shifts(zcells):
    depth = 2 * zcells
    side_x = [-4.0, 0.0, 0.0, 4.0]
    side_z = [-float(depth)] + [0.0] * zcells + [float(depth)]
    table = [[[[[side_x[ex], side_x[ey], side_z[ez]][comp] for ez in range(zcells + 2)] for ey in range(4)] for ex in range(4)] for comp in range(3)]
    return jnp.asarray(table, jnp.float32)

def block_step(table_feat, table_places, rbf_weight, radial_weight, mix_expanded, out_expanded, energy_weight, norm_expanded, reach_max, grad_table, block):
    own_feat, own_places, neigh_rows, live_counts = block
    atom_rows, slot_count = neigh_rows.shape
    channels = energy_weight.shape[0]
    coefficients = own_feat.shape[1] // channels
    degrees = radial_weight.shape[1] // channels
    edge_rows = atom_rows * slot_count
    flat_rows = neigh_rows.reshape(edge_rows)
    near_feat = jnp.take(table_feat, flat_rows, axis=0).reshape(edge_rows, coefficients, channels)
    near_places = jnp.take(table_places, flat_rows, axis=1)
    relative = near_places - jnp.repeat(own_places, slot_count, axis=1)
    distance = jnp.sqrt(lax.optimization_barrier(jnp.sum(relative * relative, axis=0)))
    nbasis = rbf_weight.shape[0]
    spacing = reach_max / (nbasis - 1)
    centred = (distance[:, None] - spacing * jnp.arange(nbasis, dtype=jnp.float32)[None, :]) / spacing
    basis_vals = jnp.exp(-0.5 * centred * centred)
    preact = product('eb,bh->eh', basis_vals.astype(jnp.bfloat16), rbf_weight)
    hidden = jax.nn.silu(preact).astype(jnp.bfloat16)
    radial = product('eh,hf->ef', hidden, radial_weight).reshape(edge_rows, degrees, channels)
    table_deg = degree_of(coefficients)
    scaled = (near_feat * radial[:, table_deg, :]).astype(jnp.bfloat16)
    mixed = product('ekc,kcd->ekd', scaled, mix_expanded)
    gating = jax.nn.sigmoid(mixed[:, :1, :])
    message = mixed * gating
    live_mask = (jnp.arange(slot_count, dtype=jnp.int32)[None, :] < live_counts[:, None]).astype(jnp.float32)
    norm_scale = 1.0 / math.sqrt(slot_count)
    summed = lax.optimization_barrier(jnp.sum(message.reshape(atom_rows, slot_count, coefficients, channels) * live_mask[:, :, None, None], axis=1)) * norm_scale
    updated = own_feat.reshape(atom_rows, coefficients, channels).astype(jnp.float32) + product('akc,kcd->akd', summed.astype(jnp.bfloat16), out_expanded)
    scalar_part = updated[:, 0, :]
    energy = lax.optimization_barrier(jnp.sum(energy_weight[None, :] * jax.nn.silu(scalar_part), axis=1)) + lax.optimization_barrier(jnp.sum(norm_expanded[None] * updated * updated, axis=(1, 2)))
    logistic = jax.nn.sigmoid(scalar_part)
    grad_updated = jnp.concatenate([(energy_weight[None, :] * logistic * (1.0 + scalar_part * (1.0 - logistic)))[:, None, :], 2.0 * norm_expanded[None, 1:, :] * updated[:, 1:, :]], axis=1)
    grad_summed = product('akd,kcd->akc', grad_updated.astype(jnp.bfloat16), out_expanded) * norm_scale
    grad_message = (grad_summed[:, None, :, :] * live_mask[:, :, None, None]).reshape(edge_rows, coefficients, channels)
    grad_first = grad_message[:, :1, :] * gating * (1.0 + mixed[:, :1, :] * (1.0 - gating)) + lax.optimization_barrier(jnp.sum(grad_message[:, 1:, :] * mixed[:, 1:, :], axis=1, keepdims=True)) * gating * (1.0 - gating)
    grad_mixed = jnp.concatenate([grad_first, grad_message[:, 1:, :] * gating], axis=1).astype(jnp.bfloat16)
    grad_scaled = product('ekd,kcd->ekc', grad_mixed, mix_expanded)
    weighted = grad_scaled * near_feat
    grad_radial = jnp.stack([lax.optimization_barrier(jnp.sum(weighted[:, degree * degree:(degree + 1) * (degree + 1), :], axis=1)) for degree in range(degrees)], axis=1)
    grad_hidden = product('ef,hf->eh', grad_radial.reshape(edge_rows, degrees * channels).astype(jnp.bfloat16), radial_weight)
    logistic_pre = jax.nn.sigmoid(preact)
    grad_preact = grad_hidden * logistic_pre * (1.0 + preact * (1.0 - logistic_pre))
    grad_basis = product('eh,bh->eb', grad_preact.astype(jnp.bfloat16), rbf_weight)
    grad_dist = lax.optimization_barrier(jnp.sum(grad_basis * basis_vals * centred, axis=1)) * (-1.0 / spacing)
    pull_vec = relative * (grad_dist / distance)[None, :]
    grad_own = -lax.optimization_barrier(jnp.sum(pull_vec.reshape(3, atom_rows, slot_count), axis=2))
    grad_table = grad_table.at[:, flat_rows].add(pull_vec)
    return (grad_table, (updated.reshape(atom_rows, coefficients * channels).astype(jnp.bfloat16), energy, grad_own))

def domain_layer(own_feat, own_places, ghost_feat, ghost_places, neigh_rows, live_counts, rbf_weight, radial_weight, mix_weight, out_weight, energy_weight, norm_weight):
    atom_rows = own_feat.shape[0]
    channels = energy_weight.shape[0]
    coefficients = own_feat.shape[1] // channels
    table_deg = degree_of(coefficients)
    mix_expanded = mix_weight[table_deg]
    out_expanded = out_weight[table_deg]
    upper_deg = table_deg[1:]
    divisor = jnp.asarray(2 * upper_deg + 1, jnp.float32)
    norm_expanded = jnp.concatenate([jnp.zeros((1, channels), jnp.float32), norm_weight[upper_deg - 1] / divisor[:, None]], axis=0)
    table_feat = jnp.concatenate([own_feat, ghost_feat], axis=0)
    table_places = jnp.concatenate([own_places, ghost_places], axis=1)
    blocks = atom_rows // 8
    layer_depth = atom_rows // 16
    reach_max = 2.0 * math.sqrt(32.0 + layer_depth * layer_depth)
    scanned = (own_feat.reshape(blocks, 8, -1), jnp.transpose(own_places.reshape(3, blocks, 8), (1, 0, 2)), neigh_rows.reshape(blocks, 8, -1), live_counts.reshape(blocks, 8))
    advance = partial(block_step, table_feat, table_places, rbf_weight, radial_weight, mix_expanded, out_expanded, energy_weight, norm_expanded, reach_max)
    grad_table, (updated, energy, grad_own) = lax.scan(advance, jnp.zeros(table_places.shape, jnp.float32), scanned)
    grad_own = jnp.transpose(grad_own, (1, 0, 2)).reshape(3, atom_rows) + grad_table[:, :atom_rows]
    return (updated.reshape(atom_rows, -1), energy.reshape(atom_rows), grad_own, grad_table[:, atom_rows:])

def fold_domains(stacked, dom_axis, ext_axis, count):
    slots = [None] * count
    for ext in range(count + 2):
        place = ext - 1
        offset = place // count
        slot = place % count
        piece = jnp.roll(lax.index_in_dim(stacked, ext, axis=ext_axis, keepdims=False), offset, axis=dom_axis)
        slots[slot] = piece if slots[slot] is None else slots[slot] + piece
    return jnp.stack(slots, axis=ext_axis)

def reference(features, positions, neighbours, counts, cell_atoms, rbf_weight, radial_weight, mix_weight, out_weight, energy_weight, norm_weight):
    span_x, span_y, span_z, atom_rows, feat = features.shape
    zcells = atom_rows // 32
    cell_feat = jnp.take_along_axis(features, cell_atoms[..., None], axis=3).reshape(span_x, span_y, span_z, 2, 2, zcells, 8, feat)
    cell_feat = jnp.transpose(cell_feat, (0, 3, 1, 4, 2, 5, 6, 7)).reshape(span_x * 2, span_y * 2, span_z * zcells, 8, feat)
    feat_pad = jnp.pad(cell_feat, ((1, 1), (1, 1), (1, 1), (0, 0), (0, 0)), mode='wrap')
    cell_places = jnp.take_along_axis(positions, cell_atoms[:, :, :, None, :], axis=4).reshape(span_x, span_y, span_z, 3, 2, 2, zcells, 8)
    cell_places = jnp.transpose(cell_places, (3, 0, 4, 1, 5, 2, 6, 7)).reshape(3, span_x * 2, span_y * 2, span_z * zcells, 8)
    places_pad = jnp.pad(cell_places, ((0, 0), (1, 1), (1, 1), (1, 1), (0, 0)), mode='wrap')
    shifts = image_shifts(zcells)
    zero = jnp.zeros((), jnp.int32)

    def per_domain(domain):
        index_x = (domain // (span_y * span_z)).astype(jnp.int32)
        index_y = (domain // span_z % span_y).astype(jnp.int32)
        index_z = (domain % span_z).astype(jnp.int32)
        ghost_feat = lax.dynamic_slice(feat_pad, (index_x * 2, index_y * 2, index_z * zcells, zero, zero), (4, 4, zcells + 2, 8, feat)).reshape(-1, feat)
        ghost_places = (lax.dynamic_slice(places_pad, (zero, index_x * 2, index_y * 2, index_z * zcells, zero), (3, 4, 4, zcells + 2, 8)) + shifts[..., None]).reshape(3, -1)
        return domain_layer(features[index_x, index_y, index_z], positions[index_x, index_y, index_z], ghost_feat, ghost_places, neighbours[index_x, index_y, index_z], counts[index_x, index_y, index_z], rbf_weight, radial_weight, mix_weight, out_weight, energy_weight, norm_weight)
    updated, energy, grad_own, grad_ghost = lax.map(per_domain, jnp.arange(span_x * span_y * span_z, dtype=jnp.int32))
    grad_ghost = grad_ghost.reshape(span_x, span_y, span_z, 3, 4, 4, zcells + 2, 8)
    folded = fold_domains(grad_ghost, 0, 4, 2)
    folded = fold_domains(folded, 1, 5, 2)
    folded = fold_domains(folded, 2, 6, zcells)
    cell_grad = folded.reshape(span_x, span_y, span_z, 3, atom_rows)
    onehot = (cell_atoms[..., :, None] == jnp.arange(atom_rows, dtype=jnp.int32)).astype(jnp.float32)
    back_own = lax.optimization_barrier(jnp.sum(cell_grad[..., :, :, None] * onehot[..., None, :, :], axis=4))
    forces = -(grad_own.reshape(span_x, span_y, span_z, 3, atom_rows) + back_own)
    return (updated.reshape(features.shape), energy.reshape(span_x, span_y, span_z, atom_rows), forces)
```

```python
from functools import partial
import math

import jax
import jax.numpy as jnp
import numpy as np
from jax import lax
from jax.experimental import pallas as pl
from jax.experimental.pallas import tpu as pltpu
from jax.sharding import PartitionSpec as P

F32, BF16 = jnp.float32, jnp.bfloat16
ATOMS, SLOTS, HALF, C, FEAT, RBF, DEGREES = 64, 32, 16, 128, 3200, 512, 5
GHOST = 512
COEFFS = FEAT // C
DEGREE = [degree for degree in range(DEGREES) for _ in range(2 * degree + 1)]
PAIRS = [tuple(range(k, min(k + 2, COEFFS))) for k in range(0, COEFFS, 2)]
BLOCKS = sorted({(DEGREE[a], DEGREE[b]) for a, b in PAIRS[:-1]})
NORM = 1.0 / math.sqrt(SLOTS)
SPACING = 2.0 * math.sqrt(48.0) / (RBF - 1)
OWN_ROWS = 256
OWN_CHUNKS = ATOMS * HALF // OWN_ROWS
GHOST_ROWS = 128
GHOST_EDGES = ATOMS * HALF
VMEM_LIMIT = 50 * 1024 * 1024


def dot(a, b):
    return lax.dot_general(a, b, (((1,), (0,)), ((), ())), preferred_element_type=F32)


def dot_nt(a, b):
    return lax.dot_general(a, b, (((1,), (1,)), ((), ())), preferred_element_type=F32)


def iota(shape, dim):
    return lax.broadcasted_iota(jnp.int32, shape, dim)


def onehot_of(hit):
    return jnp.where(hit, 1.0, 0.0).astype(BF16)


def split3(value):
    high = value.astype(BF16)
    rest = value - high.astype(F32)
    middle = rest.astype(BF16)
    return high, middle, (rest - middle.astype(F32)).astype(BF16)


def gather_places(onehot, parts, flipped):
    total = None
    for part in parts[::-1]:
        value = dot_nt(part, onehot) if flipped else dot_nt(onehot, part)
        total = value if total is None else total + value
    return total


def fill_blocks(block_ref, weight_ref):
    block_ref[...] = jnp.zeros(block_ref.shape, BF16)
    for at, (first, second) in enumerate(BLOCKS):
        block_ref[at, :C, :C] = weight_ref[first]
        block_ref[at, C:, C:] = weight_ref[second]


def pair_weight(pair, block_ref, weight_ref):
    if len(pair) == 1:
        return weight_ref[DEGREE[pair[0]]]
    return block_ref[BLOCKS.index((DEGREE[pair[0]], DEGREE[pair[1]]))]


def wide(value, pair):
    return value if len(pair) == 1 else jnp.concatenate([value, value], axis=1)


def radial_of(rel, rbf_ref, radial_ref, rad_ref, drad_ref):
    distance = jnp.sqrt(jnp.sum(rel * rel, axis=1, keepdims=True))
    rows = rel.shape[0]
    centred = distance * (1.0 / SPACING) - iota((rows, RBF), 1).astype(F32)
    basis = jnp.exp(-0.5 * centred * centred)
    preact = dot(basis.astype(BF16), rbf_ref[...])
    slope = dot((basis * centred).astype(BF16), rbf_ref[...]) * (-1.0 / SPACING)
    logistic = jax.nn.sigmoid(preact)
    hidden = (preact * logistic).astype(BF16)
    dhidden = (slope * logistic * (1.0 + preact * (1.0 - logistic))).astype(BF16)
    rad_ref[...] = dot(hidden, radial_ref[...]).astype(BF16)
    drad_ref[...] = dot(dhidden, radial_ref[...]).astype(BF16)


def edge_forward(onehot, table_ref, rad_ref, drad_ref, block_ref, mix_ref, put_message, put_slope):
    rows = onehot.shape[0]
    gate = lean = None
    for pair in PAIRS:
        lanes = slice(pair[0] * C, (pair[-1] + 1) * C)
        near = dot(onehot, table_ref[:, lanes]).astype(BF16)
        cuts = [slice(DEGREE[k] * C, (DEGREE[k] + 1) * C) for k in pair]
        rad = jnp.concatenate([rad_ref[:, cut] for cut in cuts], axis=1)
        drad = jnp.concatenate([drad_ref[:, cut] for cut in cuts], axis=1)
        both = jnp.concatenate([near * rad, near * drad], axis=0)
        both = dot(both, pair_weight(pair, block_ref, mix_ref))
        mixed, dmixed = both[:rows], both[rows:]
        if gate is None:
            gate = jax.nn.sigmoid(mixed[:, :C])
            lean = (1.0 - gate) * dmixed[:, :C]
        put_message(lanes, (mixed * wide(gate, pair)).astype(BF16))
        put_slope(lanes, ((dmixed + mixed * wide(lean, pair)) * wide(gate, pair)).astype(BF16))


def select_lane(table, lane, value):
    return jnp.sum(jnp.where(iota(table.shape, 1) == lane, table, 0.0), axis=1, keepdims=True)


def neighbour_parts(neigh_ref):
    rows = neigh_ref[...]
    return (rows >> 3).astype(F32).astype(BF16), (rows & 7).astype(F32).astype(BF16)


def own_body(
    feat_ref, pos_ref, neigh_ref, counts_ref, rbf_ref, radial_ref, mix_ref,
    acc_ref, relt_ref, pair_ref, slope_hbm,
    block_ref, pos8_ref, cells_ref, within_ref, rad_ref, drad_ref, slope_ref, sem,
):
    fill_blocks(block_ref, mix_ref)
    pos8_ref[...] = jnp.zeros(pos8_ref.shape, F32)
    pos8_ref[0:3, :] = pos_ref[...]
    parts = split3(pos8_ref[...])
    cells, within = neighbour_parts(neigh_ref)
    cells_ref[...] = cells
    within_ref[...] = within
    atoms = OWN_ROWS // HALF
    edge = iota((OWN_ROWS, 1), 0)
    spread = onehot_of(edge // HALF == iota((OWN_ROWS, atoms), 1))
    gather = onehot_of(iota((atoms, OWN_ROWS), 1) // HALF == iota((atoms, OWN_ROWS), 0))

    def copy_out(chunk):
        return pltpu.make_async_copy(
            slope_ref.at[pl.ds(chunk * OWN_ROWS, OWN_ROWS), :],
            slope_hbm.at[pl.ds(chunk * OWN_ROWS, OWN_ROWS), :],
            sem.at[chunk],
        )

    @pl.loop(0, OWN_CHUNKS)
    def _(chunk):
        here = pl.ds(pl.multiple_of(chunk * atoms, atoms), atoms)
        rows = pl.ds(pl.multiple_of(chunk * OWN_ROWS, OWN_ROWS), OWN_ROWS)
        named = dot(spread, cells_ref[here, :]) * 8.0 + dot(spread, within_ref[here, :])
        named = select_lane(named, edge % HALF, 0.0)
        centre = chunk * atoms + edge // HALF
        lane = iota((OWN_ROWS, ATOMS), 1)
        live_count = jnp.sum(jnp.where(lane == centre, counts_ref[...].astype(F32), 0.0), axis=1, keepdims=True)
        hit = lane.astype(F32) == named
        edge_pair = jnp.where(hit, 1.0, jnp.where(lane == centre, -1.0, 0.0)).astype(BF16)
        pair_ref[rows, :] = edge_pair
        relt_ref[:, rows] = gather_places(edge_pair, parts, True)
        radial_of(gather_places(edge_pair, parts, False), rbf_ref, radial_ref, rad_ref, drad_ref)
        onehot = onehot_of(jnp.logical_and(hit, (edge % HALF).astype(F32) < live_count))

        def put_message(lanes, value):
            acc_ref[here, lanes] = dot(gather, value)

        def put_slope(lanes, value):
            slope_ref[rows, lanes] = value

        edge_forward(onehot, feat_ref, rad_ref, drad_ref, block_ref, mix_ref, put_message, put_slope)
        copy_out(chunk).start()

    for chunk in range(OWN_CHUNKS):
        copy_out(chunk).wait()


def own_edges(feat, pos, neigh, counts, rbf, radial, mix):
    vmem = pl.BlockSpec(memory_space=pltpu.VMEM)
    edges = ATOMS * HALF
    return pl.pallas_call(
        own_body,
        out_shape=(
            jax.ShapeDtypeStruct((ATOMS, FEAT), F32),
            jax.ShapeDtypeStruct((8, edges), F32),
            jax.ShapeDtypeStruct((edges, ATOMS), BF16),
            jax.ShapeDtypeStruct((edges, FEAT), BF16),
        ),
        in_specs=[vmem] * 7,
        out_specs=(vmem, vmem, vmem, pl.BlockSpec(memory_space=pl.ANY)),
        scratch_shapes=[
            pltpu.VMEM((len(BLOCKS), 2 * C, 2 * C), BF16),
            pltpu.VMEM((8, ATOMS), F32),
            pltpu.VMEM((ATOMS, SLOTS), BF16),
            pltpu.VMEM((ATOMS, SLOTS), BF16),
            pltpu.VMEM((OWN_ROWS, DEGREES * C), BF16),
            pltpu.VMEM((OWN_ROWS, DEGREES * C), BF16),
            pltpu.VMEM((edges, FEAT), BF16),
            pltpu.SemaphoreType.DMA((OWN_CHUNKS,)),
        ],
        compiler_params=pltpu.CompilerParams(vmem_limit_bytes=VMEM_LIMIT),
        cost_estimate=pl.CostEstimate(flops=8_000_000_000, bytes_accessed=10_000_000, transcendentals=600_000),
        name="own_edges",
    )(feat, pos, neigh, counts, rbf, radial, mix)


def ghost_body(
    feat_ref, pos_ref, gpos_ref, neigh_ref, counts_ref, rbf_ref, radial_ref, mix_ref, out_ref,
    energy_ref, norm_ref, acc_own_ref, relt_ref, pair_ref, slope_hbm, table_hbm,
    new_ref, energies_ref, grad_own_ref, grad_ghost_ref,
    block_ref, oblock_ref, pos8_ref, gpos8_ref, cells_ref, within_ref, rad_ref, drad_ref,
    slope_ref, gslope_ref, table_ref, acc_ref, grelt_ref, gslot_ref, gatom_ref, updated_ref, gsum_ref, sem,
):
    load_table = pltpu.make_async_copy(table_hbm, table_ref, sem.at[0])
    load_slope = pltpu.make_async_copy(slope_hbm, slope_ref, sem.at[1])
    load_table.start()
    load_slope.start()
    fill_blocks(block_ref, mix_ref)
    fill_blocks(oblock_ref, out_ref)
    for target, source in ((pos8_ref, pos_ref), (gpos8_ref, gpos_ref)):
        target[...] = jnp.zeros(target.shape, F32)
        target[0:3, :] = source[...]
    parts, gparts = split3(pos8_ref[...]), split3(gpos8_ref[...])
    cells, within = neighbour_parts(neigh_ref)
    cells_ref[...] = cells
    within_ref[...] = within
    live_row = jnp.maximum(counts_ref[...].astype(F32) - float(HALF), 0.0)
    square = (ATOMS, ATOMS)
    row_id, col_id = iota(square, 0), iota(square, 1)
    live_col = jnp.sum(jnp.where(row_id == col_id, live_row, 0.0), axis=1, keepdims=True)
    start_col = jnp.sum(jnp.where(col_id < row_id, live_row, 0.0), axis=1, keepdims=True)
    start_row = jnp.sum(jnp.where(row_id < col_id, live_col, 0.0), axis=0, keepdims=True)
    total = jnp.sum(live_row).astype(jnp.int32)
    chunks = (total + GHOST_ROWS - 1) // GHOST_ROWS
    acc_ref[...] = acc_own_ref[...]
    load_table.wait()

    def spread_of(chunk):
        place = (iota((ATOMS, GHOST_ROWS), 1) + chunk * GHOST_ROWS).astype(F32)
        return jnp.logical_and(place >= start_col, place < start_col + live_col)

    @pl.loop(0, chunks)
    def _(chunk):
        rows = pl.ds(pl.multiple_of(chunk * GHOST_ROWS, GHOST_ROWS), GHOST_ROWS)
        place = (iota((GHOST_ROWS, 1), 0) + chunk * GHOST_ROWS).astype(F32)
        inside = jnp.logical_and(place >= start_row, place < start_row + live_row)
        begin = jnp.sum(jnp.where(inside, start_row, 0.0), axis=1, keepdims=True)
        spread = onehot_of(inside)
        gather = onehot_of(spread_of(chunk))
        named = dot(spread, cells_ref[...]) * 8.0 + dot(spread, within_ref[...])
        named = select_lane(named, (place - begin).astype(jnp.int32) + HALF, 0.0)
        onehot = onehot_of(iota((GHOST_ROWS, GHOST), 1).astype(F32) == named - float(ATOMS))
        gslot_ref[rows, :] = onehot
        gatom_ref[rows, :] = spread
        grelt_ref[:, rows] = gather_places(onehot, gparts, True) - gather_places(spread, parts, True)
        rel = gather_places(onehot, gparts, False) - gather_places(spread, parts, False)
        radial_of(rel, rbf_ref, radial_ref, rad_ref, drad_ref)

        def put_message(lanes, value):
            acc_ref[:, lanes] += dot(gather, value)

        def put_slope(lanes, value):
            gslope_ref[rows, lanes] = value

        edge_forward(onehot, table_ref, rad_ref, drad_ref, block_ref, mix_ref, put_message, put_slope)

    energy = None
    for pair in PAIRS:
        lanes = slice(pair[0] * C, (pair[-1] + 1) * C)
        low = (acc_ref[:, lanes] * NORM).astype(BF16)
        weight = pair_weight(pair, oblock_ref, out_ref)
        updated = feat_ref[:, lanes].astype(F32) + dot(low, weight)
        new_ref[:, lanes] = updated.astype(BF16)
        grads = []
        for at, k in enumerate(pair):
            value = updated[:, at * C : (at + 1) * C]
            if k == 0:
                logistic = jax.nn.sigmoid(value)
                scale = energy_ref[...]
                term = scale * value * logistic
                grads.append(scale * logistic * (1.0 + value * (1.0 - logistic)))
            else:
                degree = DEGREE[k]
                scaled = norm_ref[degree - 1 : degree, :] * (1.0 / (2 * degree + 1)) * value
                term = scaled * value
                grads.append(2.0 * scaled)
            energy = term if energy is None else energy + term
        grad = jnp.concatenate(grads, axis=1).astype(BF16)
        gsum_ref[:, lanes] = (dot_nt(grad, weight) * NORM).astype(BF16)
    energy = jnp.sum(energy, axis=1, keepdims=True)
    energies_ref[...] = jnp.sum(jnp.where(row_id == col_id, energy, 0.0), axis=0, keepdims=True)

    def pull_of(relt, slope_grad):
        square = jnp.sum(relt * relt, axis=0, keepdims=True)
        pull = relt * (slope_grad * jnp.where(square > 0.0, lax.rsqrt(square), 0.0))
        high = pull.astype(BF16)
        return jnp.concatenate([high, (pull - high.astype(F32)).astype(BF16)], axis=0)

    load_slope.wait()
    atoms = OWN_ROWS // HALF
    own_gather = jnp.where(iota((atoms, OWN_ROWS), 1) // HALF == iota((atoms, OWN_ROWS), 0), 1.0, 0.0)

    def own_step(chunk, total):
        here = pl.ds(pl.multiple_of(chunk * atoms, atoms), atoms)
        rows = pl.ds(pl.multiple_of(chunk * OWN_ROWS, OWN_ROWS), OWN_ROWS)
        slopes = jnp.sum(dot_nt(gsum_ref[here, :], slope_ref[rows, :]) * own_gather, axis=0, keepdims=True)
        return total + dot(pull_of(relt_ref[:, rows], slopes), pair_ref[rows, :])

    def ghost_step(chunk, totals):
        own_total, ghost_total = totals
        rows = pl.ds(pl.multiple_of(chunk * GHOST_ROWS, GHOST_ROWS), GHOST_ROWS)
        slopes = dot_nt(gsum_ref[...], gslope_ref[rows, :])
        slopes = jnp.sum(jnp.where(spread_of(chunk), slopes, 0.0), axis=0, keepdims=True)
        pull = pull_of(grelt_ref[:, rows], slopes)
        return own_total - dot(pull, gatom_ref[rows, :]), ghost_total + dot(pull, gslot_ref[rows, :])

    own_total = lax.fori_loop(0, OWN_CHUNKS, own_step, jnp.zeros((16, ATOMS), F32))
    own_total, ghost_total = lax.fori_loop(0, chunks, ghost_step, (own_total, jnp.zeros((16, GHOST), F32)))
    grad_own_ref[...] = own_total[:8] + own_total[8:]
    grad_ghost_ref[...] = ghost_total[:8] + ghost_total[8:]


def ghost_edges(*operands):
    vmem = pl.BlockSpec(memory_space=pltpu.VMEM)
    hbm = pl.BlockSpec(memory_space=pl.ANY)
    own = ATOMS * HALF
    return pl.pallas_call(
        ghost_body,
        out_shape=(
            jax.ShapeDtypeStruct((ATOMS, FEAT), BF16),
            jax.ShapeDtypeStruct((1, ATOMS), F32),
            jax.ShapeDtypeStruct((8, ATOMS), F32),
            jax.ShapeDtypeStruct((8, GHOST), F32),
        ),
        in_specs=[vmem] * 14 + [hbm] * 2,
        out_specs=(vmem,) * 4,
        scratch_shapes=[
            pltpu.VMEM((len(BLOCKS), 2 * C, 2 * C), BF16),
            pltpu.VMEM((len(BLOCKS), 2 * C, 2 * C), BF16),
            pltpu.VMEM((8, ATOMS), F32),
            pltpu.VMEM((8, GHOST), F32),
            pltpu.VMEM((ATOMS, SLOTS), BF16),
            pltpu.VMEM((ATOMS, SLOTS), BF16),
            pltpu.VMEM((GHOST_ROWS, DEGREES * C), BF16),
            pltpu.VMEM((GHOST_ROWS, DEGREES * C), BF16),
            pltpu.VMEM((own, FEAT), BF16),
            pltpu.VMEM((GHOST_EDGES, FEAT), BF16),
            pltpu.VMEM((GHOST, FEAT), BF16),
            pltpu.VMEM((ATOMS, FEAT), F32),
            pltpu.VMEM((8, GHOST_EDGES), F32),
            pltpu.VMEM((GHOST_EDGES, GHOST), BF16),
            pltpu.VMEM((GHOST_EDGES, ATOMS), BF16),
            pltpu.VMEM((8, 128), F32),
            pltpu.VMEM((ATOMS, FEAT), BF16),
            pltpu.SemaphoreType.DMA((2,)),
        ],
        compiler_params=pltpu.CompilerParams(vmem_limit_bytes=VMEM_LIMIT),
        cost_estimate=pl.CostEstimate(flops=10_000_000_000, bytes_accessed=14_000_000, transcendentals=400_000),
        name="ghost_edges",
    )(*operands)


def padded(shard, sides, width):
    for axis, dim in sides:
        peers, length = (lax.axis_size(axis), shard.shape[dim])
        up = [(i, (i + 1) % peers) for i in range(peers)]
        down = [(j, i) for i, j in up]
        last = lax.slice_in_dim(shard, length - width, length, axis=dim)
        first = lax.slice_in_dim(shard, 0, width, axis=dim)
        before = lax.ppermute(last, axis, up)
        after = lax.ppermute(first, axis, down)
        shard = jnp.concatenate([before, shard, after], axis=dim)
    return shard


def image_shifts():
    side = np.array([-4.0, 0.0, 0.0, 4.0], np.float32)
    grid = np.meshgrid(side, side, side, indexing="ij")
    return jnp.asarray(np.stack(grid), F32)


def fold_axis(received, axis):
    middle = lax.slice_in_dim(received, 2, 4, axis=axis)
    lower = lax.slice_in_dim(received, 0, 1, axis=axis)
    upper = lax.slice_in_dim(received, 5, 6, axis=axis)
    return middle + jnp.concatenate([lower, upper], axis=axis)


def domain(feat, pos, ghost_feat, ghost_places, neigh, counts, rbf, radial, mix, out, energy, norm):
    acc, relt, pairs, slopes = own_edges(feat, pos, neigh, counts, rbf, radial, mix)
    return ghost_edges(
        feat, pos, ghost_places, neigh, counts, rbf, radial, mix, out, energy, norm,
        acc, relt, pairs, slopes, ghost_feat,
    )


def local(
    features, positions, neighbours, counts, cell_atoms,
    rbf_weight, radial_weight, mix_weight, out_weight, energy_weight, norm_weight,
):
    feat = features.reshape(ATOMS, FEAT)
    pos = positions.reshape(3, ATOMS)
    order = cell_atoms.reshape(ATOMS)
    onehot = order[:, None] == jnp.arange(ATOMS, dtype=jnp.int32)[None, :]
    cell_feat = jnp.dot(onehot.astype(BF16), feat, preferred_element_type=F32).astype(BF16)
    cell_places = jnp.sum(jnp.where(onehot[None], pos[:, None, :], 0.0), axis=2)
    ghost_feat = padded(cell_feat.reshape(2, 2, 2, 8, FEAT), (("gx", 0), ("gy", 1), ("gz", 2)), 1)
    ghost_places = padded(cell_places.reshape(3, 2, 2, 2, 8), (("gx", 1), ("gy", 2), ("gz", 3)), 1)
    ghost_places = (ghost_places + image_shifts()[..., None]).reshape(3, -1)
    updated, energies, grad_own, grad_ghost = domain(
        feat, pos, ghost_feat.reshape(GHOST, FEAT), ghost_places,
        neighbours.reshape(ATOMS, SLOTS), counts.reshape(1, ATOMS),
        rbf_weight, radial_weight, mix_weight, out_weight, energy_weight.reshape(1, C), norm_weight,
    )
    grad_blocks = grad_ghost[:3].reshape(3, 4, 4, 4, 8)
    returned = padded(grad_blocks, (("gx", 1), ("gy", 2), ("gz", 3)), 1)
    cell_grad = fold_axis(fold_axis(fold_axis(returned, 1), 2), 3).reshape(3, ATOMS)
    back_own = jnp.sum(jnp.where(onehot[None], cell_grad[:, :, None], 0.0), axis=1)
    forces = -(grad_own[:3] + back_own)
    return (
        updated.reshape(features.shape),
        energies.reshape(counts.shape),
        forces.reshape(positions.shape),
    )


def solution(mesh):
    spread = P("gx", "gy", "gz", None, None)
    rows = P("gx", "gy", "gz", None)
    return jax.shard_map(
        local,
        mesh=mesh,
        in_specs=(spread, spread, spread, rows, rows) + (P(),) * 6,
        out_specs=(spread, rows, spread),
        check_vma=False,
    )
```

```python
import math

import jax
import jax.numpy as jnp
from jax import lax
from jax.experimental import pallas as pl
from jax.experimental.pallas import tpu as pltpu
from jax.sharding import PartitionSpec as P

F32, BF16 = jnp.float32, jnp.bfloat16
ATOMS, SLOTS, HALF, C, FEAT, RBF, DEGREES = 64, 32, 16, 128, 3200, 512, 5
GHOST = 512
WIDE = FEAT + C
DIRECTIONS = 27
TILES = 14
MESH_ID = pl.DeviceIdType.MESH
COEFFS = FEAT // C
DEGREE = [degree for degree in range(DEGREES) for _ in range(2 * degree + 1)]
PAIRS = [tuple(range(k, min(k + 2, COEFFS))) for k in range(0, COEFFS, 2)]
BLOCKS = sorted({(DEGREE[a], DEGREE[b]) for a, b in PAIRS[:-1]})
NORM = 1.0 / math.sqrt(SLOTS)
SPACING = 2.0 * math.sqrt(48.0) / (RBF - 1)
OWN_ROWS = 256
OWN_CHUNKS = ATOMS * HALF // OWN_ROWS
GHOST_ROWS = 128
GHOST_EDGES = ATOMS * HALF
VMEM_LIMIT = 50 * 1024 * 1024


def dot(a, b):
    return lax.dot_general(a, b, (((1,), (0,)), ((), ())), preferred_element_type=F32)


def dot_nt(a, b):
    return lax.dot_general(a, b, (((1,), (1,)), ((), ())), preferred_element_type=F32)


def iota(shape, dim):
    return lax.broadcasted_iota(jnp.int32, shape, dim)


def onehot_of(hit):
    return jnp.where(hit, 1.0, 0.0).astype(BF16)


def split3(value):
    high = value.astype(BF16)
    rest = value - high.astype(F32)
    middle = rest.astype(BF16)
    return high, middle, (rest - middle.astype(F32)).astype(BF16)


def gather_places(onehot, parts, flipped):
    total = None
    for part in parts[::-1]:
        value = dot_nt(part, onehot) if flipped else dot_nt(onehot, part)
        total = value if total is None else total + value
    return total


def fill_blocks(block_ref, weight_ref):
    block_ref[...] = jnp.zeros(block_ref.shape, BF16)
    for at, (first, second) in enumerate(BLOCKS):
        block_ref[at, :C, :C] = weight_ref[first]
        block_ref[at, C:, C:] = weight_ref[second]


def pair_weight(pair, block_ref, weight_ref):
    if len(pair) == 1:
        return weight_ref[DEGREE[pair[0]]]
    return block_ref[BLOCKS.index((DEGREE[pair[0]], DEGREE[pair[1]]))]


def wide(value, pair):
    return value if len(pair) == 1 else jnp.concatenate([value, value], axis=1)


def radial_of(rel, rbf_ref, radial_ref, rad_ref, drad_ref):
    distance = jnp.sqrt(jnp.sum(rel * rel, axis=1, keepdims=True))
    rows = rel.shape[0]
    centred = distance * (1.0 / SPACING) - iota((rows, RBF), 1).astype(F32)
    basis = jnp.exp(-0.5 * centred * centred)
    preact = dot(basis.astype(BF16), rbf_ref[...])
    slope = dot((basis * centred).astype(BF16), rbf_ref[...]) * (-1.0 / SPACING)
    logistic = jax.nn.sigmoid(preact)
    hidden = (preact * logistic).astype(BF16)
    dhidden = (slope * logistic * (1.0 + preact * (1.0 - logistic))).astype(BF16)
    rad_ref[...] = dot(hidden, radial_ref[...]).astype(BF16)
    drad_ref[...] = dot(dhidden, radial_ref[...]).astype(BF16)


def edge_forward(onehot, table_ref, rad_ref, drad_ref, block_ref, mix_ref, put_message, put_slope, last=None):
    rows = onehot.shape[0]
    gate = lean = None
    for pair in PAIRS:
        lanes = slice(pair[0] * C, (pair[-1] + 1) * C)
        if len(pair) == 1 and last is not None:
            near = last
        else:
            near = dot(onehot, table_ref[:, lanes]).astype(BF16)
        cuts = [slice(DEGREE[k] * C, (DEGREE[k] + 1) * C) for k in pair]
        rad = jnp.concatenate([rad_ref[:, cut] for cut in cuts], axis=1)
        drad = jnp.concatenate([drad_ref[:, cut] for cut in cuts], axis=1)
        both = jnp.concatenate([near * rad, near * drad], axis=0)
        both = dot(both, pair_weight(pair, block_ref, mix_ref))
        mixed, dmixed = both[:rows], both[rows:]
        if gate is None:
            gate = jax.nn.sigmoid(mixed[:, :C])
            lean = (1.0 - gate) * dmixed[:, :C]
        put_message(lanes, (mixed * wide(gate, pair)).astype(BF16))
        put_slope(lanes, ((dmixed + mixed * wide(lean, pair)) * wide(gate, pair)).astype(BF16))


def select_lane(table, lane, value):
    return jnp.sum(jnp.where(iota(table.shape, 1) == lane, table, 0.0), axis=1, keepdims=True)


def neighbour_parts(neigh_ref):
    rows = neigh_ref[...]
    return (rows >> 3).astype(F32).astype(BF16), (rows & 7).astype(F32).astype(BF16)


def column_of(row):
    square = (ATOMS, ATOMS)
    return jnp.sum(jnp.where(iota(square, 0) == iota(square, 1), row, 0.0), axis=1, keepdims=True)


def halo_copies(table_ref, send_sem, recv_sem):
    gx, gy, gz = (lax.axis_index(axis) for axis in ("gx", "gy", "gz"))
    nx, ny, nz = (lax.axis_size(axis) for axis in ("gx", "gy", "gz"))
    odd = lax.rem(gx, 2)
    sibling = (gx + 1 - 2 * odd, gy, gz)
    far = (lax.rem(gx + nx - 1 + 2 * odd, nx), gy, gz)
    down_y, up_y = ((gx, lax.rem(gy + ny + step, ny), gz) for step in (-1, 1))
    down_z, up_z = ((gx, gy, lax.rem(gz + nz + step, nz)) for step in (-1, 1))
    far_cell, shared, far_own = 3 * odd, 2 - odd, 1 + odd
    far_target, sibling_target = 3 - 3 * odd, 3 * odd
    one = lambda at: pl.ds(at, 1)
    inner, whole = pl.ds(1, 2), pl.ds(0, 4)
    plan = ([], [], [], [])

    def add(stage, device, x, y, z, to_x=None, to_y=None, to_z=None):
        at = sum(len(items) for items in plan)
        source = table_ref.at[x, y, z]
        target = table_ref.at[
            x if to_x is None else one(to_x), y if to_y is None else one(to_y), z if to_z is None else one(to_z)
        ]
        plan[stage].append(
            pltpu.make_async_remote_copy(
                src_ref=source, dst_ref=target, send_sem=send_sem.at[at], recv_sem=recv_sem.at[at],
                device_id=device, device_id_type=MESH_ID,
            )
        )

    ends = ((down_z, 1, 3), (up_z, 2, 0))
    add(0, far, one(far_own), inner, inner, to_x=far_target)
    add(0, down_y, inner, one(1), inner, to_y=3)
    add(0, up_y, inner, one(2), inner, to_y=0)
    for device, at, to in ends:
        add(0, device, inner, inner, one(at), to_z=to)
    add(0, sibling, one(shared), inner, inner, to_x=sibling_target)
    add(1, down_y, one(far_cell), one(1), inner, to_y=3)
    add(1, up_y, one(far_cell), one(2), inner, to_y=0)
    for edge in (0, 3):
        for device, at, to in ends:
            add(1, device, inner, one(edge), one(at), to_z=to)
    for device, at, to in ends:
        add(1, device, one(far_cell), inner, one(at), to_z=to)
    for edge in (0, 3):
        add(1, sibling, one(shared), one(edge), inner, to_x=sibling_target)
    for edge in (0, 3):
        for device, at, to in ends:
            add(2, device, one(far_cell), one(edge), one(at), to_z=to)
    for edge in (0, 3):
        add(3, sibling, one(shared), whole, one(edge), to_x=sibling_target)
    return plan, (sibling, far, down_y, up_y, down_z, up_z)


HALO_COPIES = 22


def own_body(
    feat_ref, pos_ref, neigh_ref, counts_ref, order_ref, rbf_ref, radial_ref, mix_ref,
    acc_ref, relt_ref, pair_ref, table_ref, slope_hbm,
    block_ref, pos8_ref, cells_ref, within_ref, rad_ref, drad_ref, slope_ref, sem, send_sem, recv_sem,
):
    plan, devices = halo_copies(table_ref, send_sem, recv_sem)
    barrier = pltpu.get_barrier_semaphore()
    for device in devices:
        pl.semaphore_signal(barrier, inc=1, device_id=device, device_id_type=MESH_ID)
    pos8_ref[...] = jnp.zeros(pos8_ref.shape, F32)
    pos8_ref[0:3, :] = pos_ref[...]
    parts = split3(pos8_ref[...])
    listed = column_of(order_ref[...].astype(F32)) == iota((ATOMS, ATOMS), 1).astype(F32)
    listed = onehot_of(listed)
    box = (2, 2, 2, 8)
    for start in range(0, FEAT, 2 * C):
        lanes = slice(start, min(start + 2 * C, FEAT))
        value = dot(listed, feat_ref[:, lanes])
        table_ref[1:3, 1:3, 1:3, :, lanes] = value.reshape(box + (value.shape[1],)).astype(BF16)
    stacked = [part.astype(F32) for part in parts] + [jnp.zeros((C - 24, ATOMS), F32)]
    value = dot_nt(listed, jnp.concatenate(stacked, axis=0).astype(BF16))
    table_ref[1:3, 1:3, 1:3, :, FEAT:] = value.reshape(box + (C,)).astype(BF16)
    pl.semaphore_wait(barrier, len(devices))
    for copy in plan[0]:
        copy.start()
    fill_blocks(block_ref, mix_ref)
    cells, within = neighbour_parts(neigh_ref)
    cells_ref[...] = cells
    within_ref[...] = within
    atoms = OWN_ROWS // HALF
    edge = iota((OWN_ROWS, 1), 0)
    spread = onehot_of(edge // HALF == iota((OWN_ROWS, atoms), 1))
    gather = onehot_of(iota((atoms, OWN_ROWS), 1) // HALF == iota((atoms, OWN_ROWS), 0))

    def copy_out(chunk):
        return pltpu.make_async_copy(
            slope_ref.at[pl.ds(chunk * OWN_ROWS, OWN_ROWS), :],
            slope_hbm.at[pl.ds(chunk * OWN_ROWS, OWN_ROWS), :],
            sem.at[chunk],
        )

    @pl.loop(0, OWN_CHUNKS)
    def _(chunk):
        here = pl.ds(pl.multiple_of(chunk * atoms, atoms), atoms)
        rows = pl.ds(pl.multiple_of(chunk * OWN_ROWS, OWN_ROWS), OWN_ROWS)
        named = dot(spread, cells_ref[here, :]) * 8.0 + dot(spread, within_ref[here, :])
        named = select_lane(named, edge % HALF, 0.0)
        centre = chunk * atoms + edge // HALF
        lane = iota((OWN_ROWS, ATOMS), 1)
        live_count = jnp.sum(jnp.where(lane == centre, counts_ref[...].astype(F32), 0.0), axis=1, keepdims=True)
        hit = lane.astype(F32) == named
        edge_pair = jnp.where(hit, 1.0, jnp.where(lane == centre, -1.0, 0.0)).astype(BF16)
        pair_ref[rows, :] = edge_pair
        relt_ref[:, rows] = gather_places(edge_pair, parts, True)
        radial_of(gather_places(edge_pair, parts, False), rbf_ref, radial_ref, rad_ref, drad_ref)
        onehot = onehot_of(jnp.logical_and(hit, (edge % HALF).astype(F32) < live_count))

        def put_message(lanes, value):
            acc_ref[here, lanes] = dot(gather, value)

        def put_slope(lanes, value):
            slope_ref[rows, lanes] = value

        edge_forward(onehot, feat_ref, rad_ref, drad_ref, block_ref, mix_ref, put_message, put_slope)
        copy_out(chunk).start()

        @pl.when(chunk == 0)
        def _():
            for at in (0, 1, 2):
                plan[0][at].wait_recv()
            for copy in plan[1]:
                copy.start()

        @pl.when(chunk == 1)
        def _():
            for at in (0, 1):
                plan[1][at].wait_recv()
            for copy in plan[2]:
                copy.start()

        @pl.when(chunk == 2)
        def _():
            for copy in (plan[0][3], plan[0][4]) + tuple(plan[1][2:6]):
                copy.wait_recv()
            for copy in plan[3]:
                copy.start()

    for copy in [plan[0][5]] + plan[1][6:] + plan[2] + plan[3]:
        copy.wait_recv()
    for items in plan:
        for copy in items:
            copy.wait_send()
    for chunk in range(OWN_CHUNKS):
        copy_out(chunk).wait()


def own_edges(feat, pos, neigh, counts, order, rbf, radial, mix):
    vmem = pl.BlockSpec(memory_space=pltpu.VMEM)
    edges = ATOMS * HALF
    return pl.pallas_call(
        own_body,
        out_shape=(
            jax.ShapeDtypeStruct((ATOMS, FEAT), F32),
            jax.ShapeDtypeStruct((8, edges), F32),
            jax.ShapeDtypeStruct((edges, ATOMS), BF16),
            jax.ShapeDtypeStruct((4, 4, 4, 8, WIDE), BF16),
            jax.ShapeDtypeStruct((edges, FEAT), BF16),
        ),
        in_specs=[vmem] * 8,
        out_specs=(vmem, vmem, vmem, vmem, pl.BlockSpec(memory_space=pl.ANY)),
        scratch_shapes=[
            pltpu.VMEM((len(BLOCKS), 2 * C, 2 * C), BF16),
            pltpu.VMEM((8, ATOMS), F32),
            pltpu.VMEM((ATOMS, SLOTS), BF16),
            pltpu.VMEM((ATOMS, SLOTS), BF16),
            pltpu.VMEM((OWN_ROWS, DEGREES * C), BF16),
            pltpu.VMEM((OWN_ROWS, DEGREES * C), BF16),
            pltpu.VMEM((edges, FEAT), BF16),
            pltpu.SemaphoreType.DMA((OWN_CHUNKS,)),
            pltpu.SemaphoreType.DMA((HALO_COPIES,)),
            pltpu.SemaphoreType.DMA((HALO_COPIES,)),
        ],
        compiler_params=pltpu.CompilerParams(vmem_limit_bytes=VMEM_LIMIT, collective_id=0, has_side_effects=True),
        cost_estimate=pl.CostEstimate(flops=8_000_000_000, bytes_accessed=10_000_000, transcendentals=600_000),
        name="own_edges",
    )(feat, pos, neigh, counts, order, rbf, radial, mix)


def ghost_body(
    feat_ref, pos_ref, neigh_ref, counts_ref, rbf_ref, radial_ref, mix_ref, out_ref,
    energy_ref, norm_ref, acc_own_ref, relt_ref, pair_ref, table_ref, slope_hbm,
    new_ref, energies_ref, grad_own_ref, tiles_ref,
    block_ref, oblock_ref, pos8_ref, cells_ref, within_ref, rad_ref, drad_ref,
    slope_ref, gslope_ref, acc_ref, grelt_ref, gslot_ref, gatom_ref, gsum_ref, sem,
):
    load_slope = pltpu.make_async_copy(slope_hbm, slope_ref, sem)
    load_slope.start()
    fill_blocks(block_ref, mix_ref)
    fill_blocks(oblock_ref, out_ref)
    pos8_ref[...] = jnp.zeros(pos8_ref.shape, F32)
    pos8_ref[0:3, :] = pos_ref[...]
    stacked = [part.astype(F32) for part in split3(pos8_ref[...])] + [jnp.zeros((C - 24, ATOMS), F32)]
    stacked = jnp.concatenate(stacked, axis=0).astype(BF16)
    cells, within = neighbour_parts(neigh_ref)
    cells_ref[...] = cells
    within_ref[...] = within
    live_row = jnp.maximum(counts_ref[...].astype(F32) - float(HALF), 0.0)
    square = (ATOMS, ATOMS)
    row_id, col_id = iota(square, 0), iota(square, 1)
    live_col = jnp.sum(jnp.where(row_id == col_id, live_row, 0.0), axis=1, keepdims=True)
    start_col = jnp.sum(jnp.where(col_id < row_id, live_row, 0.0), axis=1, keepdims=True)
    start_row = jnp.sum(jnp.where(row_id < col_id, live_col, 0.0), axis=0, keepdims=True)
    total = jnp.sum(live_row).astype(jnp.int32)
    chunks = (total + GHOST_ROWS - 1) // GHOST_ROWS
    acc_ref[...] = acc_own_ref[...]

    def whole(gathered):
        return gathered + (pltpu.roll(gathered, C - 8, 1) + pltpu.roll(gathered, C - 16, 1))

    def spread_of(chunk):
        place = (iota((ATOMS, GHOST_ROWS), 1) + chunk * GHOST_ROWS).astype(F32)
        return jnp.logical_and(place >= start_col, place < start_col + live_col)

    @pl.loop(0, chunks)
    def _(chunk):
        rows = pl.ds(pl.multiple_of(chunk * GHOST_ROWS, GHOST_ROWS), GHOST_ROWS)
        place = (iota((GHOST_ROWS, 1), 0) + chunk * GHOST_ROWS).astype(F32)
        inside = jnp.logical_and(place >= start_row, place < start_row + live_row)
        begin = jnp.sum(jnp.where(inside, start_row, 0.0), axis=1, keepdims=True)
        spread = onehot_of(inside)
        gather = onehot_of(spread_of(chunk))
        named = dot(spread, cells_ref[...]) * 8.0 + dot(spread, within_ref[...])
        named = select_lane(named, (place - begin).astype(jnp.int32) + HALF, 0.0)
        onehot = onehot_of(iota((GHOST_ROWS, GHOST), 1).astype(F32) == named - float(ATOMS))
        row = named.astype(jnp.int32) - ATOMS
        inside = row >= 0
        row = jnp.maximum(row, 0)
        spots = [(row >> shift) & 3 for shift in (7, 5, 3)]
        moves = [jnp.where(spot == 0, -1, jnp.where(spot == 3, 1, 0)) for spot in spots]
        toward = moves[0] * 9 + moves[1] * 3 + moves[2] + 13
        slot = row & 7
        for at, spot in enumerate(spots):
            slot = slot + (((spot + 1) & 1) << (5 - at))
        place = jnp.where(inside, toward * ATOMS + slot, -1)
        gslot_ref[rows, :] = onehot_of(iota((GHOST_ROWS, TILES * C), 1) == place)
        gatom_ref[rows, :] = spread
        lane = iota((GHOST_ROWS, C), 1)
        last = dot(onehot, table_ref[:, FEAT - C :])
        image = jnp.zeros((GHOST_ROWS, C), F32)
        for at, move in enumerate(moves):
            image = jnp.where(lane == at, move.astype(F32) * 4.0, image)
        rel = (whole(last[:, C:]) + image) - whole(dot_nt(spread, stacked))
        rel = jnp.where(jnp.logical_and(lane < 3, inside), rel, 0.0)
        grelt_ref[:, rows] = rel.T[:8]
        radial_of(rel, rbf_ref, radial_ref, rad_ref, drad_ref)

        def put_message(lanes, value):
            acc_ref[:, lanes] += dot(gather, value)

        def put_slope(lanes, value):
            gslope_ref[rows, lanes] = value

        last = last[:, :C].astype(BF16)
        edge_forward(onehot, table_ref, rad_ref, drad_ref, block_ref, mix_ref, put_message, put_slope, last)

    energy = None
    for pair in PAIRS:
        lanes = slice(pair[0] * C, (pair[-1] + 1) * C)
        low = (acc_ref[:, lanes] * NORM).astype(BF16)
        weight = pair_weight(pair, oblock_ref, out_ref)
        updated = feat_ref[:, lanes].astype(F32) + dot(low, weight)
        new_ref[:, lanes] = updated.astype(BF16)
        grads = []
        for at, k in enumerate(pair):
            value = updated[:, at * C : (at + 1) * C]
            if k == 0:
                logistic = jax.nn.sigmoid(value)
                scale = energy_ref[...]
                term = scale * value * logistic
                grads.append(scale * logistic * (1.0 + value * (1.0 - logistic)))
            else:
                degree = DEGREE[k]
                scaled = norm_ref[degree - 1 : degree, :] * (1.0 / (2 * degree + 1)) * value
                term = scaled * value
                grads.append(2.0 * scaled)
            energy = term if energy is None else energy + term
        grad = jnp.concatenate(grads, axis=1).astype(BF16)
        gsum_ref[:, lanes] = (dot_nt(grad, weight) * NORM).astype(BF16)
    energy = jnp.sum(energy, axis=1, keepdims=True)
    energies_ref[...] = jnp.sum(jnp.where(row_id == col_id, energy, 0.0), axis=0, keepdims=True)

    def pull_of(relt, slope_grad):
        square = jnp.sum(relt * relt, axis=0, keepdims=True)
        pull = relt * (slope_grad * jnp.where(square > 0.0, lax.rsqrt(square), 0.0))
        high = pull.astype(BF16)
        return jnp.concatenate([high, (pull - high.astype(F32)).astype(BF16)], axis=0)

    load_slope.wait()
    atoms = OWN_ROWS // HALF
    own_gather = jnp.where(iota((atoms, OWN_ROWS), 1) // HALF == iota((atoms, OWN_ROWS), 0), 1.0, 0.0)

    def own_step(chunk, total):
        here = pl.ds(pl.multiple_of(chunk * atoms, atoms), atoms)
        rows = pl.ds(pl.multiple_of(chunk * OWN_ROWS, OWN_ROWS), OWN_ROWS)
        slopes = jnp.sum(dot_nt(gsum_ref[here, :], slope_ref[rows, :]) * own_gather, axis=0, keepdims=True)
        return total + dot(pull_of(relt_ref[:, rows], slopes), pair_ref[rows, :])

    def ghost_step(chunk, totals):
        own_total, ghost_total = totals
        rows = pl.ds(pl.multiple_of(chunk * GHOST_ROWS, GHOST_ROWS), GHOST_ROWS)
        slopes = dot_nt(gsum_ref[...], gslope_ref[rows, :])
        slopes = jnp.sum(jnp.where(spread_of(chunk), slopes, 0.0), axis=0, keepdims=True)
        pull = pull_of(grelt_ref[:, rows], slopes)
        return own_total - dot(pull, gatom_ref[rows, :]), ghost_total + dot(pull, gslot_ref[rows, :])

    own_total = lax.fori_loop(0, OWN_CHUNKS, own_step, jnp.zeros((16, ATOMS), F32))
    own_total, ghost_total = lax.fori_loop(0, chunks, ghost_step, (own_total, jnp.zeros((16, TILES * C), F32)))
    grad_own_ref[...] = own_total[:8] + own_total[8:]
    for tile in range(TILES):
        lanes = slice(tile * C, (tile + 1) * C)
        tiles_ref[tile] = ghost_total[:8, lanes] + ghost_total[8:, lanes]


def ghost_edges(*operands):
    vmem = pl.BlockSpec(memory_space=pltpu.VMEM)
    hbm = pl.BlockSpec(memory_space=pl.ANY)
    own = ATOMS * HALF
    return pl.pallas_call(
        ghost_body,
        out_shape=(
            jax.ShapeDtypeStruct((ATOMS, FEAT), BF16),
            jax.ShapeDtypeStruct((1, ATOMS), F32),
            jax.ShapeDtypeStruct((8, ATOMS), F32),
            jax.ShapeDtypeStruct((TILES, 8, C), F32),
        ),
        in_specs=[vmem] * 14 + [hbm],
        out_specs=(vmem,) * 4,
        scratch_shapes=[
            pltpu.VMEM((len(BLOCKS), 2 * C, 2 * C), BF16),
            pltpu.VMEM((len(BLOCKS), 2 * C, 2 * C), BF16),
            pltpu.VMEM((8, ATOMS), F32),
            pltpu.VMEM((ATOMS, SLOTS), BF16),
            pltpu.VMEM((ATOMS, SLOTS), BF16),
            pltpu.VMEM((GHOST_ROWS, DEGREES * C), BF16),
            pltpu.VMEM((GHOST_ROWS, DEGREES * C), BF16),
            pltpu.VMEM((own, FEAT), BF16),
            pltpu.VMEM((GHOST_EDGES, FEAT), BF16),
            pltpu.VMEM((ATOMS, FEAT), F32),
            pltpu.VMEM((8, GHOST_EDGES), F32),
            pltpu.VMEM((GHOST_EDGES, TILES * C), BF16),
            pltpu.VMEM((GHOST_EDGES, ATOMS), BF16),
            pltpu.VMEM((ATOMS, FEAT), BF16),
            pltpu.SemaphoreType.DMA,
        ],
        compiler_params=pltpu.CompilerParams(vmem_limit_bytes=VMEM_LIMIT),
        cost_estimate=pl.CostEstimate(flops=10_000_000_000, bytes_accessed=14_000_000, transcendentals=400_000),
        name="ghost_edges",
    )(*operands)


def return_body(tiles_ref, grad_own_ref, order_ref, forces_ref, landed_ref, send_sem, recv_sem):
    here = [lax.axis_index(axis) for axis in ("gx", "gy", "gz")]
    sizes = [lax.axis_size(axis) for axis in ("gx", "gy", "gz")]
    barrier = pltpu.get_barrier_semaphore()
    others = [at for at in range(DIRECTIONS) if at != DIRECTIONS // 2]
    copies = []
    for at in others:
        moves = (at // 9 - 1, at // 3 % 3 - 1, at % 3 - 1)
        device = tuple(lax.rem(h + n + m, n) for h, n, m in zip(here, sizes, moves))
        pl.semaphore_signal(barrier, inc=1, device_id=device, device_id_type=MESH_ID)
        copies.append(
            pltpu.make_async_remote_copy(
                src_ref=tiles_ref.at[at // 2], dst_ref=landed_ref.at[at],
                send_sem=send_sem.at[at], recv_sem=recv_sem.at[at],
                device_id=device, device_id_type=MESH_ID,
            )
        )
    pl.semaphore_wait(barrier, len(others))
    for copy in copies:
        copy.start()
    listed = column_of(order_ref[...].astype(F32)) == iota((ATOMS, ATOMS), 1).astype(F32)
    listed = onehot_of(listed)
    for copy in copies:
        copy.wait_recv()
    even = sum(landed_ref[at] for at in others if at % 2 == 0)
    odd = sum(landed_ref[at] for at in others if at % 2 == 1)
    total = (even + pltpu.roll(odd, ATOMS, 1))[:, :ATOMS]
    back = sum(dot(part, listed) for part in split3(total)[::-1])
    forces_ref[...] = -(grad_own_ref[...] + back)[:3]
    for copy in copies:
        copy.wait_send()


def return_forces(tiles, grad_own, order):
    vmem = pl.BlockSpec(memory_space=pltpu.VMEM)
    return pl.pallas_call(
        return_body,
        out_shape=jax.ShapeDtypeStruct((3, ATOMS), F32),
        in_specs=[vmem] * 3,
        out_specs=vmem,
        scratch_shapes=[
            pltpu.VMEM((DIRECTIONS, 8, C), F32),
            pltpu.SemaphoreType.DMA((DIRECTIONS,)),
            pltpu.SemaphoreType.DMA((DIRECTIONS,)),
        ],
        compiler_params=pltpu.CompilerParams(collective_id=1, has_side_effects=True),
        name="return_forces",
    )(tiles, grad_own, order)


def local(
    features, positions, neighbours, counts, cell_atoms,
    rbf_weight, radial_weight, mix_weight, out_weight, energy_weight, norm_weight,
):
    feat = features.reshape(ATOMS, FEAT)
    pos = positions.reshape(3, ATOMS)
    neigh = neighbours.reshape(ATOMS, SLOTS)
    live = counts.reshape(1, ATOMS)
    order = cell_atoms.reshape(1, ATOMS)
    acc, relt, pairs, table, slopes = own_edges(feat, pos, neigh, live, order, rbf_weight, radial_weight, mix_weight)
    updated, energies, grad_own, tiles = ghost_edges(
        feat, pos, neigh, live, rbf_weight, radial_weight, mix_weight, out_weight,
        energy_weight.reshape(1, C), norm_weight, acc, relt, pairs, table.reshape(GHOST, WIDE), slopes,
    )
    forces = return_forces(tiles, grad_own, order)
    return (
        updated.reshape(features.shape),
        energies.reshape(counts.shape),
        forces.reshape(positions.shape),
    )


def solution(mesh):
    spread = P("gx", "gy", "gz", None, None)
    rows = P("gx", "gy", "gz", None)
    return jax.shard_map(
        local,
        mesh=mesh,
        in_specs=(spread, spread, spread, rows, rows) + (P(),) * 6,
        out_specs=(spread, rows, spread),
        check_vma=False,
    )
```

```python
import math

import jax
import jax.numpy as jnp
from jax import lax
from jax.experimental import pallas as pl
from jax.experimental.pallas import tpu as pltpu
from jax.sharding import PartitionSpec as P

F32, BF16 = jnp.float32, jnp.bfloat16
ATOMS, SLOTS, HALF, C, FEAT, RBF, DEGREES = 64, 32, 16, 128, 3200, 512, 5
GHOST = 512
WIDE = FEAT + C
DIRECTIONS = 27
TILES = 14
MESH_ID = pl.DeviceIdType.MESH
COEFFS = FEAT // C
DEGREE = [degree for degree in range(DEGREES) for _ in range(2 * degree + 1)]
PAIRS = [tuple(range(k, min(k + 2, COEFFS))) for k in range(0, COEFFS, 2)]
BLOCKS = sorted({(DEGREE[a], DEGREE[b]) for a, b in PAIRS[:-1]})
NORM = 1.0 / math.sqrt(SLOTS)
SPACING = 2.0 * math.sqrt(48.0) / (RBF - 1)
OWN_ROWS = 256
OWN_CHUNKS = ATOMS * HALF // OWN_ROWS
GHOST_ROWS = 128
GHOST_EDGES = ATOMS * HALF
VMEM_LIMIT = 50 * 1024 * 1024


def dot(a, b):
    return lax.dot_general(a, b, (((1,), (0,)), ((), ())), preferred_element_type=F32)


def dot_nt(a, b):
    return lax.dot_general(a, b, (((1,), (1,)), ((), ())), preferred_element_type=F32)


def iota(shape, dim):
    return lax.broadcasted_iota(jnp.int32, shape, dim)


def onehot_of(hit):
    return jnp.where(hit, 1.0, 0.0).astype(BF16)


def split3(value):
    high = value.astype(BF16)
    rest = value - high.astype(F32)
    middle = rest.astype(BF16)
    return high, middle, (rest - middle.astype(F32)).astype(BF16)


def gather_places(onehot, parts, flipped):
    total = None
    for part in parts[::-1]:
        value = dot_nt(part, onehot) if flipped else dot_nt(onehot, part)
        total = value if total is None else total + value
    return total


def fill_blocks(block_ref, weight_ref):
    block_ref[...] = jnp.zeros(block_ref.shape, BF16)
    for at, (first, second) in enumerate(BLOCKS):
        block_ref[at, :C, :C] = weight_ref[first]
        block_ref[at, C:, C:] = weight_ref[second]


def pair_weight(pair, block_ref, weight_ref):
    if len(pair) == 1:
        return weight_ref[DEGREE[pair[0]]]
    return block_ref[BLOCKS.index((DEGREE[pair[0]], DEGREE[pair[1]]))]


def wide(value, pair):
    return value if len(pair) == 1 else jnp.concatenate([value, value], axis=1)


def radial_of(rel, rbf_ref, radial_ref, rad_ref, drad_ref):
    distance = jnp.sqrt(jnp.sum(rel * rel, axis=1, keepdims=True))
    rows = rel.shape[0]
    centred = distance * (1.0 / SPACING) - iota((rows, RBF), 1).astype(F32)
    basis = jnp.exp(-0.5 * centred * centred)
    preact = dot(basis.astype(BF16), rbf_ref[...])
    slope = dot((basis * centred).astype(BF16), rbf_ref[...]) * (-1.0 / SPACING)
    logistic = jax.nn.sigmoid(preact)
    hidden = (preact * logistic).astype(BF16)
    dhidden = (slope * logistic * (1.0 + preact * (1.0 - logistic))).astype(BF16)
    rad_ref[...] = dot(hidden, radial_ref[...]).astype(BF16)
    drad_ref[...] = dot(dhidden, radial_ref[...]).astype(BF16)


def edge_forward(onehot, table_ref, rad_ref, drad_ref, block_ref, mix_ref, lhs_ref, message_ref, put_slope, last=None, middle=None):
    rows = onehot.shape[0]
    for pair in PAIRS:
        lanes = slice(pair[0] * C, (pair[-1] + 1) * C)
        if len(pair) == 1 and last is not None:
            near = last
        else:
            near = dot(onehot, table_ref[:, lanes]).astype(BF16)
        for at, k in enumerate(pair):
            cut = slice(DEGREE[k] * C, (DEGREE[k] + 1) * C)
            half = near[:, at * C : (at + 1) * C]
            lhs_ref[:rows, k * C : (k + 1) * C] = half * rad_ref[:, cut]
            lhs_ref[rows:, k * C : (k + 1) * C] = half * drad_ref[:, cut]
    if middle is not None:
        middle()
    gate = lean = None
    for pair in PAIRS:
        lanes = slice(pair[0] * C, (pair[-1] + 1) * C)
        both = dot(lhs_ref[:, lanes], pair_weight(pair, block_ref, mix_ref))
        mixed, dmixed = both[:rows], both[rows:]
        if gate is None:
            gate = jax.nn.sigmoid(mixed[:, :C])
            lean = (1.0 - gate) * dmixed[:, :C]
        message_ref[:, lanes] = (mixed * wide(gate, pair)).astype(BF16)
        put_slope(lanes, ((dmixed + mixed * wide(lean, pair)) * wide(gate, pair)).astype(BF16))


def select_lane(table, lane, value):
    return jnp.sum(jnp.where(iota(table.shape, 1) == lane, table, 0.0), axis=1, keepdims=True)


def neighbour_parts(neigh_ref):
    rows = neigh_ref[...]
    return (rows >> 3).astype(F32).astype(BF16), (rows & 7).astype(F32).astype(BF16)


def column_of(row):
    square = (ATOMS, ATOMS)
    return jnp.sum(jnp.where(iota(square, 0) == iota(square, 1), row, 0.0), axis=1, keepdims=True)


def halo_copies(table_ref, send_sem, recv_sem):
    gx, gy, gz = (lax.axis_index(axis) for axis in ("gx", "gy", "gz"))
    nx, ny, nz = (lax.axis_size(axis) for axis in ("gx", "gy", "gz"))
    odd = lax.rem(gx, 2)
    sibling = (gx + 1 - 2 * odd, gy, gz)
    far = (lax.rem(gx + nx - 1 + 2 * odd, nx), gy, gz)
    down_y, up_y = ((gx, lax.rem(gy + ny + step, ny), gz) for step in (-1, 1))
    down_z, up_z = ((gx, gy, lax.rem(gz + nz + step, nz)) for step in (-1, 1))
    far_cell, shared, far_own = 3 * odd, 2 - odd, 1 + odd
    far_target, sibling_target = 3 - 3 * odd, 3 * odd
    one = lambda at: pl.ds(at, 1)
    inner, whole = pl.ds(1, 2), pl.ds(0, 4)
    plan = {}

    def add(name, device, x, y, z, to_x=None, to_y=None, to_z=None):
        at = len(plan)
        source = table_ref.at[x, y, z]
        target = table_ref.at[
            x if to_x is None else one(to_x), y if to_y is None else one(to_y), z if to_z is None else one(to_z)
        ]
        plan[name] = pltpu.make_async_remote_copy(
            src_ref=source, dst_ref=target, send_sem=send_sem.at[at], recv_sem=recv_sem.at[at],
            device_id=device, device_id_type=MESH_ID,
        )

    add("far", far, one(far_own), inner, inner, to_x=far_target)
    for x, kind in ((inner, "own"), (one(far_cell), "far")):
        add(kind + "_yd_a", down_y, x, one(1), one(1), to_y=3)
        add(kind + "_yu_a", up_y, x, one(2), one(2), to_y=0)
        add(kind + "_zd_a", down_z, x, one(2), one(1), to_z=3)
        add(kind + "_zu_a", up_z, x, one(1), one(2), to_z=0)
        add(kind + "_yd_b", down_y, x, one(1), one(2), to_y=3)
        add(kind + "_yu_b", up_y, x, one(2), one(1), to_y=0)
        add(kind + "_zd_b", down_z, x, one(1), one(1), to_z=3)
        add(kind + "_zu_b", up_z, x, one(2), one(2), to_z=0)
        add(kind + "_zd_e", down_z, x, one(3), one(1), to_z=3)
        add(kind + "_zu_e", up_z, x, one(0), one(2), to_z=0)
        add(kind + "_yd_e", down_y, x, one(1), one(0), to_y=3)
        add(kind + "_yu_e", up_y, x, one(2), one(3), to_y=0)
    add("sib", sibling, one(shared), inner, inner, to_x=sibling_target)
    for edge in (0, 3):
        add("sib_y%d" % edge, sibling, one(shared), one(edge), inner, to_x=sibling_target)
        add("sib_z%d" % edge, sibling, one(shared), inner, one(edge), to_x=sibling_target)
        add("sib_e%d0" % edge, sibling, one(shared), one(edge), one(0), to_x=sibling_target)
        add("sib_e%d3" % edge, sibling, one(shared), one(edge), one(3), to_x=sibling_target)
    return plan, (sibling, far, down_y, up_y, down_z, up_z)


def halo_steps(plan):
    sides = ("_yd", "_yu", "_zd", "_zu")
    names = lambda kind, piece: [kind + side + piece for side in sides]
    steps = (
        ([], ["far"] + names("own", "_a") + names("own", "_b") + ["sib"]),
        (names("own", "_a"), names("own", "_e")),
        (["far"], names("far", "_a") + names("far", "_b")),
        (names("own", "_b"), ["sib_y0", "sib_y3", "sib_z0", "sib_z3"]),
        (names("far", "_a"), names("far", "_e")),
        (names("own", "_e"), ["sib_e00", "sib_e03", "sib_e30", "sib_e33"]),
        (names("far", "_b") + names("far", "_e") + [name for name in plan if name.startswith("sib")], []),
    )

    def run(step):
        for name in steps[step][0]:
            plan[name].wait_recv()
        for name in steps[step][1]:
            plan[name].start()

    return run


HALO_COPIES = 34


def load_all(sources, targets, sem):
    copies = [pltpu.make_async_copy(a, b, sem.at[at]) for at, (a, b) in enumerate(zip(sources, targets))]
    for copy in copies:
        copy.start()
    return copies


def like(operands):
    return [pltpu.VMEM(operand.shape, operand.dtype) for operand in operands] + [
        pltpu.SemaphoreType.DMA((len(operands),))
    ]


def own_body(
    feat_hbm, pos_hbm, neigh_hbm, counts_hbm, order_hbm, rbf_hbm, radial_hbm, mix_hbm, out_hbm,
    acc_ref, relt_ref, pair_ref, table_ref, block_ref, oblock_ref, slope_hbm,
    feat_ref, pos_ref, neigh_ref, counts_ref, order_ref, rbf_ref, radial_ref, mix_ref, out_ref, load_sem,
    pos8_ref, cells_ref, within_ref, rad_ref, drad_ref, lhs_ref, message_ref, slope_ref, sem, send_sem, recv_sem,
):
    loads = load_all(
        (feat_hbm, pos_hbm, neigh_hbm, counts_hbm, order_hbm, rbf_hbm, radial_hbm, mix_hbm, out_hbm),
        (feat_ref, pos_ref, neigh_ref, counts_ref, order_ref, rbf_ref, radial_ref, mix_ref, out_ref),
        load_sem,
    )
    plan, devices = halo_copies(table_ref, send_sem, recv_sem)
    barrier = pltpu.get_barrier_semaphore()
    for device in devices:
        pl.semaphore_signal(barrier, inc=1, device_id=device, device_id_type=MESH_ID)
    pos8_ref[...] = jnp.zeros(pos8_ref.shape, F32)
    for at in (0, 1, 4):
        loads[at].wait()
    pos8_ref[0:3, :] = pos_ref[:, 0, :]
    parts = split3(pos8_ref[...])
    listed = column_of(order_ref[...].astype(F32)) == iota((ATOMS, ATOMS), 1).astype(F32)
    listed = onehot_of(listed)
    box = (2, 2, 2, 8)
    for start in range(0, FEAT, 2 * C):
        lanes = slice(start, min(start + 2 * C, FEAT))
        value = dot(listed, feat_ref[:, lanes])
        table_ref[1:3, 1:3, 1:3, :, lanes] = value.reshape(box + (value.shape[1],)).astype(BF16)
    stacked = [part.astype(F32) for part in parts] + [jnp.zeros((C - 24, ATOMS), F32)]
    value = dot_nt(listed, jnp.concatenate(stacked, axis=0).astype(BF16))
    table_ref[1:3, 1:3, 1:3, :, FEAT:] = value.reshape(box + (C,)).astype(BF16)
    for at in (7, 8):
        loads[at].wait()
    fill_blocks(block_ref, mix_ref)
    fill_blocks(oblock_ref, out_ref)
    advance = halo_steps(plan)
    pl.semaphore_wait(barrier, len(devices))
    advance(0)
    for at in (2, 3, 5, 6):
        loads[at].wait()
    cells, within = neighbour_parts(neigh_ref)
    cells_ref[...] = cells
    within_ref[...] = within
    atoms = OWN_ROWS // HALF
    edge = iota((OWN_ROWS, 1), 0)
    gather = onehot_of(iota((atoms, OWN_ROWS), 1) // HALF == iota((atoms, OWN_ROWS), 0))

    def copy_out(chunk):
        return pltpu.make_async_copy(
            slope_ref.at[pl.ds(chunk * OWN_ROWS, OWN_ROWS), :],
            slope_hbm.at[pl.ds(chunk * OWN_ROWS, OWN_ROWS), :],
            sem.at[chunk],
        )

    @pl.loop(0, OWN_CHUNKS)
    def _(chunk):
        here = pl.ds(pl.multiple_of(chunk * atoms, atoms), atoms)
        rows = pl.ds(pl.multiple_of(chunk * OWN_ROWS, OWN_ROWS), OWN_ROWS)
        centre = chunk * atoms + edge // HALF
        lane = iota((OWN_ROWS, ATOMS), 1)
        spread = onehot_of(lane == centre)
        named = dot_nt(spread, cells_ref[...]) * 8.0 + dot_nt(spread, within_ref[...])
        named = select_lane(named, edge % HALF, 0.0)
        live_count = jnp.sum(jnp.where(lane == centre, counts_ref[...].astype(F32), 0.0), axis=1, keepdims=True)
        hit = lane.astype(F32) == named
        edge_pair = jnp.where(hit, 1.0, jnp.where(lane == centre, -1.0, 0.0)).astype(BF16)
        pair_ref[rows, :] = edge_pair
        relt_ref[:, rows] = gather_places(edge_pair, parts, True)
        radial_of(gather_places(edge_pair, parts, False), rbf_ref, radial_ref, rad_ref, drad_ref)
        onehot = onehot_of(jnp.logical_and(hit, (edge % HALF).astype(F32) < live_count))

        def put_slope(lanes, value):
            slope_ref[rows, lanes] = value

        def middle():
            for at, step in ((1, 1), (3, 5)):
                @pl.when(chunk == at)
                def _():
                    advance(step)

        edge_forward(onehot, feat_ref, rad_ref, drad_ref, block_ref, mix_ref, lhs_ref, message_ref, put_slope, middle=middle)
        for pair in PAIRS:
            lanes = slice(pair[0] * C, (pair[-1] + 1) * C)
            acc_ref[here, lanes] = dot(gather, message_ref[:, lanes])
        copy_out(chunk).start()

        for at, steps in ((1, (2, 3)), (2, (4,))):
            @pl.when(chunk == at)
            def _():
                for step in steps:
                    advance(step)

    advance(6)
    for copy in plan.values():
        copy.wait_send()
    for chunk in range(OWN_CHUNKS):
        copy_out(chunk).wait()


def own_edges(*operands):
    vmem = pl.BlockSpec(memory_space=pltpu.VMEM)
    edges = ATOMS * HALF
    return pl.pallas_call(
        own_body,
        out_shape=(
            jax.ShapeDtypeStruct((ATOMS, FEAT), F32),
            jax.ShapeDtypeStruct((8, edges), F32),
            jax.ShapeDtypeStruct((edges, ATOMS), BF16),
            jax.ShapeDtypeStruct((4, 4, 4, 8, WIDE), BF16),
            jax.ShapeDtypeStruct((len(BLOCKS), 2 * C, 2 * C), BF16),
            jax.ShapeDtypeStruct((len(BLOCKS), 2 * C, 2 * C), BF16),
            jax.ShapeDtypeStruct((edges, FEAT), BF16),
        ),
        in_specs=[pl.BlockSpec(memory_space=pltpu.HBM)] * len(operands),
        out_specs=(vmem,) * 6 + (pl.BlockSpec(memory_space=pl.ANY),),
        scratch_shapes=like(operands)
        + [
            pltpu.VMEM((8, ATOMS), F32),
            pltpu.VMEM((SLOTS, ATOMS), BF16),
            pltpu.VMEM((SLOTS, ATOMS), BF16),
            pltpu.VMEM((OWN_ROWS, DEGREES * C), BF16),
            pltpu.VMEM((OWN_ROWS, DEGREES * C), BF16),
            pltpu.VMEM((2 * OWN_ROWS, FEAT), BF16),
            pltpu.VMEM((OWN_ROWS, FEAT), BF16),
            pltpu.VMEM((edges, FEAT), BF16),
            pltpu.SemaphoreType.DMA((OWN_CHUNKS,)),
            pltpu.SemaphoreType.DMA((HALO_COPIES,)),
            pltpu.SemaphoreType.DMA((HALO_COPIES,)),
        ],
        compiler_params=pltpu.CompilerParams(vmem_limit_bytes=VMEM_LIMIT, collective_id=0, has_side_effects=True),
        cost_estimate=pl.CostEstimate(flops=8_000_000_000, bytes_accessed=10_000_000, transcendentals=600_000),
        name="own_edges",
    )(*operands)


def ghost_body(
    feat_hbm, pos_hbm, neigh_hbm, counts_hbm, rbf_hbm, radial_hbm, mix_hbm, out_hbm,
    energy_hbm, norm_hbm, acc_own_ref, relt_ref, pair_ref, table_ref, block_ref, oblock_ref, slope_hbm,
    new_ref, energies_ref, grad_own_ref, tiles_ref,
    feat_ref, pos_ref, neigh_ref, counts_ref, rbf_ref, radial_ref, mix_ref, out_ref,
    energy_ref, norm_ref, load_sem,
    pos8_ref, cells_ref, within_ref, rad_ref, drad_ref, lhs_ref, message_ref,
    slope_ref, gslope_ref, acc_ref, grelt_ref, gslot_ref, gatom_ref, updated_ref, grad_ref, gsum_ref, sem,
):
    loads = load_all(
        (pos_hbm, neigh_hbm, counts_hbm, rbf_hbm, radial_hbm, mix_hbm, out_hbm, feat_hbm, energy_hbm, norm_hbm),
        (pos_ref, neigh_ref, counts_ref, rbf_ref, radial_ref, mix_ref, out_ref, feat_ref, energy_ref, norm_ref),
        load_sem,
    )
    load_slope = pltpu.make_async_copy(slope_hbm, slope_ref, sem)
    load_slope.start()
    for at in (0, 1, 2):
        loads[at].wait()
    pos8_ref[...] = jnp.zeros(pos8_ref.shape, F32)
    pos8_ref[0:3, :] = pos_ref[:, 0, :]
    stacked = [part.astype(F32) for part in split3(pos8_ref[...])] + [jnp.zeros((C - 24, ATOMS), F32)]
    stacked = jnp.concatenate(stacked, axis=0).astype(BF16)
    cells, within = neighbour_parts(neigh_ref)
    cells_ref[...] = cells
    within_ref[...] = within
    live_row = jnp.maximum(counts_ref[...].astype(F32) - float(HALF), 0.0)
    square = (ATOMS, ATOMS)
    row_id, col_id = iota(square, 0), iota(square, 1)
    live_col = jnp.sum(jnp.where(row_id == col_id, live_row, 0.0), axis=1, keepdims=True)
    start_col = jnp.sum(jnp.where(col_id < row_id, live_row, 0.0), axis=1, keepdims=True)
    start_row = jnp.sum(jnp.where(row_id < col_id, live_col, 0.0), axis=0, keepdims=True)
    total = jnp.sum(live_row).astype(jnp.int32)
    chunks = (total + GHOST_ROWS - 1) // GHOST_ROWS
    acc_ref[...] = acc_own_ref[...]
    for copy in loads[3:]:
        copy.wait()

    def whole(gathered):
        return gathered + (pltpu.roll(gathered, C - 8, 1) + pltpu.roll(gathered, C - 16, 1))

    def spread_of(chunk):
        place = (iota((ATOMS, GHOST_ROWS), 1) + chunk * GHOST_ROWS).astype(F32)
        return jnp.logical_and(place >= start_col, place < start_col + live_col)

    @pl.loop(0, chunks)
    def _(chunk):
        rows = pl.ds(pl.multiple_of(chunk * GHOST_ROWS, GHOST_ROWS), GHOST_ROWS)
        place = (iota((GHOST_ROWS, 1), 0) + chunk * GHOST_ROWS).astype(F32)
        inside = jnp.logical_and(place >= start_row, place < start_row + live_row)
        begin = jnp.sum(jnp.where(inside, start_row, 0.0), axis=1, keepdims=True)
        spread = onehot_of(inside)
        gather = onehot_of(spread_of(chunk))
        named = dot_nt(spread, cells_ref[...]) * 8.0 + dot_nt(spread, within_ref[...])
        named = select_lane(named, (place - begin).astype(jnp.int32) + HALF, 0.0)
        onehot = onehot_of(iota((GHOST_ROWS, GHOST), 1).astype(F32) == named - float(ATOMS))
        row = named.astype(jnp.int32) - ATOMS
        inside = row >= 0
        row = jnp.maximum(row, 0)
        spots = [(row >> shift) & 3 for shift in (7, 5, 3)]
        moves = [jnp.where(spot == 0, -1, jnp.where(spot == 3, 1, 0)) for spot in spots]
        toward = moves[0] * 9 + moves[1] * 3 + moves[2] + 13
        slot = row & 7
        for at, spot in enumerate(spots):
            slot = slot + (((spot + 1) & 1) << (5 - at))
        place = jnp.where(inside, toward * ATOMS + slot, -1)
        gslot_ref[rows, :] = onehot_of(iota((GHOST_ROWS, TILES * C), 1) == place)
        gatom_ref[rows, :] = spread
        lane = iota((GHOST_ROWS, C), 1)
        last = dot(onehot, table_ref[:, FEAT - C :])
        image = jnp.zeros((GHOST_ROWS, C), F32)
        for at, move in enumerate(moves):
            image = jnp.where(lane == at, move.astype(F32) * 4.0, image)
        rel = (whole(last[:, C:]) + image) - whole(dot_nt(spread, stacked))
        rel = jnp.where(jnp.logical_and(lane < 3, inside), rel, 0.0)
        grelt_ref[:, rows] = rel.T[:8]
        radial_of(rel, rbf_ref, radial_ref, rad_ref, drad_ref)

        def put_slope(lanes, value):
            gslope_ref[rows, lanes] = value

        last = last[:, :C].astype(BF16)
        edge_forward(onehot, table_ref, rad_ref, drad_ref, block_ref, mix_ref, lhs_ref, message_ref, put_slope, last)
        for pair in PAIRS:
            lanes = slice(pair[0] * C, (pair[-1] + 1) * C)
            acc_ref[:, lanes] += dot(gather, message_ref[:, lanes])

    for pair in PAIRS:
        lanes = slice(pair[0] * C, (pair[-1] + 1) * C)
        low = (acc_ref[:, lanes] * NORM).astype(BF16)
        updated_ref[:, lanes] = dot(low, pair_weight(pair, oblock_ref, out_ref))
    energy = None
    for k in range(COEFFS):
        lanes = slice(k * C, (k + 1) * C)
        value = feat_ref[:, lanes].astype(F32) + updated_ref[:, lanes]
        new_ref[:, lanes] = value.astype(BF16)
        if k == 0:
            logistic = jax.nn.sigmoid(value)
            scale = energy_ref[...]
            term = scale * value * logistic
            grad = scale * logistic * (1.0 + value * (1.0 - logistic))
        else:
            degree = DEGREE[k]
            scaled = norm_ref[degree - 1 : degree, :] * (1.0 / (2 * degree + 1)) * value
            term = scaled * value
            grad = 2.0 * scaled
        energy = term if energy is None else energy + term
        grad_ref[:, lanes] = grad.astype(BF16)
    for pair in PAIRS:
        lanes = slice(pair[0] * C, (pair[-1] + 1) * C)
        weight = pair_weight(pair, oblock_ref, out_ref)
        gsum_ref[:, lanes] = (dot_nt(grad_ref[:, lanes], weight) * NORM).astype(BF16)
    energy = jnp.sum(energy, axis=1, keepdims=True)
    energies_ref[...] = jnp.sum(jnp.where(row_id == col_id, energy, 0.0), axis=0, keepdims=True)

    def pull_of(relt, slope_grad):
        square = jnp.sum(relt * relt, axis=0, keepdims=True)
        pull = relt * (slope_grad * jnp.where(square > 0.0, lax.rsqrt(square), 0.0))
        high = pull.astype(BF16)
        return jnp.concatenate([high, (pull - high.astype(F32)).astype(BF16)], axis=0)

    load_slope.wait()

    def own_step(chunk, total):
        rows = pl.ds(pl.multiple_of(chunk * OWN_ROWS, OWN_ROWS), OWN_ROWS)
        slopes = dot_nt(slope_ref[rows, :], gsum_ref[...]).T
        own = (iota((ATOMS, OWN_ROWS), 1) + chunk * OWN_ROWS) // HALF == iota((ATOMS, OWN_ROWS), 0)
        slopes = jnp.sum(jnp.where(own, slopes, 0.0), axis=0, keepdims=True)
        return total + dot(pull_of(relt_ref[:, rows], slopes), pair_ref[rows, :])

    def ghost_step(chunk, totals):
        own_total, ghost_total = totals
        rows = pl.ds(pl.multiple_of(chunk * GHOST_ROWS, GHOST_ROWS), GHOST_ROWS)
        slopes = dot_nt(gslope_ref[rows, :], gsum_ref[...]).T
        slopes = jnp.sum(jnp.where(spread_of(chunk), slopes, 0.0), axis=0, keepdims=True)
        pull = pull_of(grelt_ref[:, rows], slopes)
        return own_total - dot(pull, gatom_ref[rows, :]), ghost_total + dot(pull, gslot_ref[rows, :])

    own_total = lax.fori_loop(0, OWN_CHUNKS, own_step, jnp.zeros((16, ATOMS), F32))
    own_total, ghost_total = lax.fori_loop(0, chunks, ghost_step, (own_total, jnp.zeros((16, TILES * C), F32)))
    grad_own_ref[...] = own_total[:8] + own_total[8:]
    for tile in range(TILES):
        lanes = slice(tile * C, (tile + 1) * C)
        tiles_ref[tile] = ghost_total[:8, lanes] + ghost_total[8:, lanes]


def ghost_edges(*operands):
    vmem = pl.BlockSpec(memory_space=pltpu.VMEM)
    hbm = pl.BlockSpec(memory_space=pl.ANY)
    own = ATOMS * HALF
    return pl.pallas_call(
        ghost_body,
        out_shape=(
            jax.ShapeDtypeStruct((ATOMS, FEAT), BF16),
            jax.ShapeDtypeStruct((1, ATOMS), F32),
            jax.ShapeDtypeStruct((8, ATOMS), F32),
            jax.ShapeDtypeStruct((TILES, 8, C), F32),
        ),
        in_specs=[pl.BlockSpec(memory_space=pltpu.HBM)] * 10 + [vmem] * 6 + [hbm],
        out_specs=(vmem,) * 4,
        scratch_shapes=like(operands[:10])
        + [
            pltpu.VMEM((8, ATOMS), F32),
            pltpu.VMEM((SLOTS, ATOMS), BF16),
            pltpu.VMEM((SLOTS, ATOMS), BF16),
            pltpu.VMEM((GHOST_ROWS, DEGREES * C), BF16),
            pltpu.VMEM((GHOST_ROWS, DEGREES * C), BF16),
            pltpu.VMEM((2 * GHOST_ROWS, FEAT), BF16),
            pltpu.VMEM((GHOST_ROWS, FEAT), BF16),
            pltpu.VMEM((own, FEAT), BF16),
            pltpu.VMEM((GHOST_EDGES, FEAT), BF16),
            pltpu.VMEM((ATOMS, FEAT), F32),
            pltpu.VMEM((8, GHOST_EDGES), F32),
            pltpu.VMEM((GHOST_EDGES, TILES * C), BF16),
            pltpu.VMEM((GHOST_EDGES, ATOMS), BF16),
            pltpu.VMEM((ATOMS, FEAT), F32),
            pltpu.VMEM((ATOMS, FEAT), BF16),
            pltpu.VMEM((ATOMS, FEAT), BF16),
            pltpu.SemaphoreType.DMA,
        ],
        compiler_params=pltpu.CompilerParams(vmem_limit_bytes=VMEM_LIMIT),
        cost_estimate=pl.CostEstimate(flops=10_000_000_000, bytes_accessed=14_000_000, transcendentals=400_000),
        name="ghost_edges",
    )(*operands)


def return_body(tiles_ref, grad_own_ref, order_hbm, forces_ref, order_ref, load_sem, landed_ref, send_sem, recv_sem):
    loads = load_all((order_hbm,), (order_ref,), load_sem)
    here = [lax.axis_index(axis) for axis in ("gx", "gy", "gz")]
    sizes = [lax.axis_size(axis) for axis in ("gx", "gy", "gz")]
    barrier = pltpu.get_barrier_semaphore()
    others = [at for at in range(DIRECTIONS) if at != DIRECTIONS // 2]
    copies = []
    for at in others:
        moves = (at // 9 - 1, at // 3 % 3 - 1, at % 3 - 1)
        device = tuple(lax.rem(h + n + m, n) for h, n, m in zip(here, sizes, moves))
        pl.semaphore_signal(barrier, inc=1, device_id=device, device_id_type=MESH_ID)
        copies.append(
            pltpu.make_async_remote_copy(
                src_ref=tiles_ref.at[at // 2], dst_ref=landed_ref.at[at],
                send_sem=send_sem.at[at], recv_sem=recv_sem.at[at],
                device_id=device, device_id_type=MESH_ID,
            )
        )
    pl.semaphore_wait(barrier, len(others))
    for copy in copies:
        copy.start()
    loads[0].wait()
    listed = column_of(order_ref[...].astype(F32)) == iota((ATOMS, ATOMS), 1).astype(F32)
    listed = onehot_of(listed)
    for copy in copies:
        copy.wait_recv()
    even = sum(landed_ref[at] for at in others if at % 2 == 0)
    odd = sum(landed_ref[at] for at in others if at % 2 == 1)
    total = (even + pltpu.roll(odd, ATOMS, 1))[:, :ATOMS]
    back = sum(dot(part, listed) for part in split3(total)[::-1])
    forces_ref[:, 0, :] = -(grad_own_ref[...] + back)[:3]
    for copy in copies:
        copy.wait_send()


def return_forces(tiles, grad_own, order):
    vmem = pl.BlockSpec(memory_space=pltpu.VMEM)
    return pl.pallas_call(
        return_body,
        out_shape=jax.ShapeDtypeStruct((3, 1, ATOMS), F32),
        in_specs=[vmem] * 2 + [pl.BlockSpec(memory_space=pltpu.HBM)],
        out_specs=vmem,
        scratch_shapes=like((order,))
        + [
            pltpu.VMEM((DIRECTIONS, 8, C), F32),
            pltpu.SemaphoreType.DMA((DIRECTIONS,)),
            pltpu.SemaphoreType.DMA((DIRECTIONS,)),
        ],
        compiler_params=pltpu.CompilerParams(collective_id=1, has_side_effects=True, vmem_limit_bytes=4 * 1024 * 1024),
        name="return_forces",
    )(tiles, grad_own, order)


def local(
    features, positions, neighbours, counts, cell_atoms,
    rbf_weight, radial_weight, mix_weight, out_weight, energy_weight, norm_weight,
):
    feat = features.reshape(ATOMS, FEAT)
    pos = positions.reshape(3, 1, ATOMS)
    neigh = jnp.transpose(neighbours.reshape(ATOMS, SLOTS))
    live = counts.reshape(1, ATOMS)
    order = cell_atoms.reshape(1, ATOMS)
    energy, norm = energy_weight.reshape(1, C), norm_weight
    feat, pos, neigh, live, order, rbf_weight, radial_weight, mix_weight, out_weight, energy, norm = (
        pltpu.with_memory_space_constraint(operand, pltpu.HBM)
        for operand in (feat, pos, neigh, live, order, rbf_weight, radial_weight, mix_weight, out_weight, energy, norm)
    )
    acc, relt, pairs, table, blocks, oblocks, slopes = own_edges(
        feat, pos, neigh, live, order, rbf_weight, radial_weight, mix_weight, out_weight
    )
    updated, energies, grad_own, tiles = ghost_edges(
        feat, pos, neigh, live, rbf_weight, radial_weight, mix_weight, out_weight,
        energy, norm, acc, relt, pairs, table.reshape(GHOST, WIDE), blocks, oblocks, slopes,
    )
    forces = return_forces(tiles, grad_own, order)
    return (
        updated.reshape(features.shape),
        energies.reshape(counts.shape),
        forces.reshape(positions.shape),
    )


def solution(mesh):
    spread = P("gx", "gy", "gz", None, None)
    rows = P("gx", "gy", "gz", None)
    return jax.shard_map(
        local,
        mesh=mesh,
        in_specs=(spread, spread, spread, rows, rows) + (P(),) * 6,
        out_specs=(spread, rows, spread),
        check_vma=False,
    )
```

```python
import math

import jax
import jax.numpy as jnp
from jax import lax
from jax.experimental import pallas as pl
from jax.experimental.pallas import tpu as pltpu
from jax.sharding import PartitionSpec as P

F32, BF16 = jnp.float32, jnp.bfloat16
ATOMS, SLOTS, HALF, C, FEAT, RBF, DEGREES = 64, 32, 16, 128, 3200, 512, 5
GHOST = 512
WIDE = FEAT + C
DIRECTIONS = 27
TILES = 14
MESH_ID = pl.DeviceIdType.MESH
COEFFS = FEAT // C
DEGREE = [degree for degree in range(DEGREES) for _ in range(2 * degree + 1)]
PAIRS = [tuple(range(k, min(k + 2, COEFFS))) for k in range(0, COEFFS, 2)]
BLOCKS = sorted({(DEGREE[a], DEGREE[b]) for a, b in PAIRS[:-1]})
NORM = 1.0 / math.sqrt(SLOTS)
SPACING = 2.0 * math.sqrt(48.0) / (RBF - 1)
OWN_ROWS = 256
OWN_CHUNKS = ATOMS * HALF // OWN_ROWS
GHOST_ROWS = 128
HEAD = 512
TAIL = 256
GHOST_EDGES = ATOMS * HALF
VMEM_LIMIT = 50 * 1024 * 1024


def dot(a, b):
    return lax.dot_general(a, b, (((1,), (0,)), ((), ())), preferred_element_type=F32)


def dot_nt(a, b):
    return lax.dot_general(a, b, (((1,), (1,)), ((), ())), preferred_element_type=F32)


def iota(shape, dim):
    return lax.broadcasted_iota(jnp.int32, shape, dim)


def onehot_of(hit):
    return jnp.where(hit, 1.0, 0.0).astype(BF16)


def split3(value):
    high = value.astype(BF16)
    rest = value - high.astype(F32)
    middle = rest.astype(BF16)
    return high, middle, (rest - middle.astype(F32)).astype(BF16)


def gather_places(onehot, parts, flipped):
    total = None
    for part in parts[::-1]:
        value = dot_nt(part, onehot) if flipped else dot_nt(onehot, part)
        total = value if total is None else total + value
    return total


def fill_blocks(block_ref, weight_ref):
    block_ref[...] = jnp.zeros(block_ref.shape, BF16)
    for at, (first, second) in enumerate(BLOCKS):
        block_ref[at, :C, :C] = weight_ref[first]
        block_ref[at, C:, C:] = weight_ref[second]


def pair_weight(pair, block_ref, weight_ref):
    if len(pair) == 1:
        return weight_ref[DEGREE[pair[0]]]
    return block_ref[BLOCKS.index((DEGREE[pair[0]], DEGREE[pair[1]]))]


def wide(value, pair):
    return value if len(pair) == 1 else jnp.concatenate([value, value], axis=1)


def radial_of(rel, rbf_ref, radial_ref, rad_ref, drad_ref, at):
    distance = jnp.sqrt(jnp.sum(rel * rel, axis=1, keepdims=True))
    rows = rel.shape[0]
    centred = distance * (1.0 / SPACING) - iota((rows, RBF), 1).astype(F32)
    basis = jnp.exp(-0.5 * centred * centred)
    preact = dot(basis.astype(BF16), rbf_ref[...])
    slope = dot((basis * centred).astype(BF16), rbf_ref[...]) * (-1.0 / SPACING)
    logistic = jax.nn.sigmoid(preact)
    hidden = (preact * logistic).astype(BF16)
    dhidden = (slope * logistic * (1.0 + preact * (1.0 - logistic))).astype(BF16)
    rad_ref[at, :] = dot(hidden, radial_ref[...]).astype(BF16)
    drad_ref[at, :] = dot(dhidden, radial_ref[...]).astype(BF16)


def edge_forward(onehot, table_ref, rad_ref, drad_ref, at_rows, block_ref, mix_ref, lhs_ref, message_ref, put_slope, last=None, middle=None):
    rows = onehot.shape[0]
    for pair in PAIRS:
        lanes = slice(pair[0] * C, (pair[-1] + 1) * C)
        if len(pair) == 1 and last is not None:
            near = last
        else:
            near = dot(onehot, table_ref[:, lanes]).astype(BF16)
        for at, k in enumerate(pair):
            cut = slice(DEGREE[k] * C, (DEGREE[k] + 1) * C)
            half = near[:, at * C : (at + 1) * C]
            lhs_ref[:rows, k * C : (k + 1) * C] = half * rad_ref[at_rows, cut]
            lhs_ref[rows:, k * C : (k + 1) * C] = half * drad_ref[at_rows, cut]
    if middle is not None:
        middle()
    gate = lean = None
    for pair in PAIRS:
        lanes = slice(pair[0] * C, (pair[-1] + 1) * C)
        both = dot(lhs_ref[:, lanes], pair_weight(pair, block_ref, mix_ref))
        mixed, dmixed = both[:rows], both[rows:]
        if gate is None:
            gate = jax.nn.sigmoid(mixed[:, :C])
            lean = (1.0 - gate) * dmixed[:, :C]
        message_ref[:, lanes] = (mixed * wide(gate, pair)).astype(BF16)
        put_slope(lanes, ((dmixed + mixed * wide(lean, pair)) * wide(gate, pair)).astype(BF16))


def select_lane(table, lane, value):
    return jnp.sum(jnp.where(iota(table.shape, 1) == lane, table, 0.0), axis=1, keepdims=True)


def neighbour_parts(neigh_ref):
    rows = neigh_ref[...]
    return (rows >> 3).astype(F32).astype(BF16), (rows & 7).astype(F32).astype(BF16)


def column_of(row):
    square = (ATOMS, ATOMS)
    return jnp.sum(jnp.where(iota(square, 0) == iota(square, 1), row, 0.0), axis=1, keepdims=True)


def halo_copies(table_ref, send_sem, recv_sem):
    gx, gy, gz = (lax.axis_index(axis) for axis in ("gx", "gy", "gz"))
    nx, ny, nz = (lax.axis_size(axis) for axis in ("gx", "gy", "gz"))
    odd = lax.rem(gx, 2)
    sibling = (gx + 1 - 2 * odd, gy, gz)
    far = (lax.rem(gx + nx - 1 + 2 * odd, nx), gy, gz)
    down_y, up_y = ((gx, lax.rem(gy + ny + step, ny), gz) for step in (-1, 1))
    down_z, up_z = ((gx, gy, lax.rem(gz + nz + step, nz)) for step in (-1, 1))
    far_cell, shared, far_own = 3 * odd, 2 - odd, 1 + odd
    far_target, sibling_target = 3 - 3 * odd, 3 * odd
    one = lambda at: pl.ds(at, 1)
    inner, whole = pl.ds(1, 2), pl.ds(0, 4)
    plan = {}

    def add(name, device, x, y, z, to_x=None, to_y=None, to_z=None):
        at = len(plan)
        source = table_ref.at[x, y, z]
        target = table_ref.at[
            x if to_x is None else one(to_x), y if to_y is None else one(to_y), z if to_z is None else one(to_z)
        ]
        plan[name] = pltpu.make_async_remote_copy(
            src_ref=source, dst_ref=target, send_sem=send_sem.at[at], recv_sem=recv_sem.at[at],
            device_id=device, device_id_type=MESH_ID,
        )

    add("far", far, one(far_own), inner, inner, to_x=far_target)
    for x, kind in ((inner, "own"), (one(far_cell), "far")):
        add(kind + "_yd_a", down_y, x, one(1), one(1), to_y=3)
        add(kind + "_yu_a", up_y, x, one(2), one(2), to_y=0)
        add(kind + "_zd_a", down_z, x, one(2), one(1), to_z=3)
        add(kind + "_zu_a", up_z, x, one(1), one(2), to_z=0)
        add(kind + "_yd_b", down_y, x, one(1), one(2), to_y=3)
        add(kind + "_yu_b", up_y, x, one(2), one(1), to_y=0)
        add(kind + "_zd_b", down_z, x, one(1), one(1), to_z=3)
        add(kind + "_zu_b", up_z, x, one(2), one(2), to_z=0)
        add(kind + "_zd_e", down_z, x, one(3), one(1), to_z=3)
        add(kind + "_zu_e", up_z, x, one(0), one(2), to_z=0)
        add(kind + "_yd_e", down_y, x, one(1), one(0), to_y=3)
        add(kind + "_yu_e", up_y, x, one(2), one(3), to_y=0)
    add("sib", sibling, one(shared), inner, inner, to_x=sibling_target)
    for edge in (0, 3):
        add("sib_y%d" % edge, sibling, one(shared), one(edge), inner, to_x=sibling_target)
        add("sib_z%d" % edge, sibling, one(shared), inner, one(edge), to_x=sibling_target)
        add("sib_e%d0" % edge, sibling, one(shared), one(edge), one(0), to_x=sibling_target)
        add("sib_e%d3" % edge, sibling, one(shared), one(edge), one(3), to_x=sibling_target)
    return plan, (sibling, far, down_y, up_y, down_z, up_z)


def halo_steps(plan):
    sides = ("_yd", "_yu", "_zd", "_zu")
    names = lambda kind, piece: [kind + side + piece for side in sides]
    steps = (
        ([], ["far"] + names("own", "_a") + names("own", "_b") + ["sib"]),
        (names("own", "_a"), names("own", "_e")),
        (["far"], names("far", "_a") + names("far", "_b")),
        (names("own", "_b"), ["sib_y0", "sib_y3", "sib_z0", "sib_z3"]),
        (names("far", "_a"), names("far", "_e")),
        (names("own", "_e"), ["sib_e00", "sib_e03", "sib_e30", "sib_e33"]),
        (names("far", "_b") + names("far", "_e") + [name for name in plan if name.startswith("sib")], []),
    )

    def run(step):
        for name in steps[step][0]:
            plan[name].wait_recv()
        for name in steps[step][1]:
            plan[name].start()

    return run


HALO_COPIES = 34


def load_all(sources, targets, sem):
    copies = [pltpu.make_async_copy(a, b, sem.at[at]) for at, (a, b) in enumerate(zip(sources, targets))]
    for copy in copies:
        copy.start()
    return copies


def like(operands):
    return [pltpu.VMEM(operand.shape, operand.dtype) for operand in operands] + [
        pltpu.SemaphoreType.DMA((len(operands),))
    ]


def own_body(
    feat_hbm, pos_hbm, neigh_hbm, counts_hbm, order_hbm, rbf_hbm, radial_hbm, mix_hbm, out_hbm,
    acc_ref, relt_ref, pair_ref, table_ref, block_ref, oblock_ref, slope_hbm,
    feat_ref, pos_ref, neigh_ref, counts_ref, order_ref, rbf_ref, radial_ref, mix_ref, out_ref, load_sem,
    pos8_ref, cells_ref, within_ref, rad_ref, drad_ref, hot_ref, lhs_ref, message_ref, slope_ref, sem, send_sem, recv_sem,
):
    loads = load_all(
        (feat_hbm, pos_hbm, neigh_hbm, counts_hbm, order_hbm, rbf_hbm, radial_hbm, mix_hbm, out_hbm),
        (feat_ref, pos_ref, neigh_ref, counts_ref, order_ref, rbf_ref, radial_ref, mix_ref, out_ref),
        load_sem,
    )
    plan, devices = halo_copies(table_ref, send_sem, recv_sem)
    barrier = pltpu.get_barrier_semaphore()
    for device in devices:
        pl.semaphore_signal(barrier, inc=1, device_id=device, device_id_type=MESH_ID)
    pos8_ref[...] = jnp.zeros(pos8_ref.shape, F32)
    for at in (0, 1, 4):
        loads[at].wait()
    pos8_ref[0:3, :] = pos_ref[:, 0, :]
    parts = split3(pos8_ref[...])
    listed = column_of(order_ref[...].astype(F32)) == iota((ATOMS, ATOMS), 1).astype(F32)
    listed = onehot_of(listed)
    box = (2, 2, 2, 8)
    for start in range(0, FEAT, 2 * C):
        lanes = slice(start, min(start + 2 * C, FEAT))
        value = dot(listed, feat_ref[:, lanes])
        table_ref[1:3, 1:3, 1:3, :, lanes] = value.reshape(box + (value.shape[1],)).astype(BF16)
    stacked = [part.astype(F32) for part in parts] + [jnp.zeros((C - 24, ATOMS), F32)]
    value = dot_nt(listed, jnp.concatenate(stacked, axis=0).astype(BF16))
    table_ref[1:3, 1:3, 1:3, :, FEAT:] = value.reshape(box + (C,)).astype(BF16)
    for at in (7, 8):
        loads[at].wait()
    fill_blocks(block_ref, mix_ref)
    fill_blocks(oblock_ref, out_ref)
    advance = halo_steps(plan)
    pl.semaphore_wait(barrier, len(devices))
    advance(0)
    for at in (2, 3, 5, 6):
        loads[at].wait()
    cells, within = neighbour_parts(neigh_ref)
    cells_ref[...] = cells
    within_ref[...] = within
    atoms = OWN_ROWS // HALF
    gather = onehot_of(iota((atoms, OWN_ROWS), 1) // HALF == iota((atoms, OWN_ROWS), 0))

    def copy_out(chunk):
        return pltpu.make_async_copy(
            slope_ref.at[pl.ds(chunk * OWN_ROWS, OWN_ROWS), :],
            slope_hbm.at[pl.ds(chunk * OWN_ROWS, OWN_ROWS), :],
            sem.at[chunk],
        )

    def geometry(start, count):
        rows = slice(start, start + count)
        edge = iota((count, 1), 0)
        centre = (start + edge) // HALF
        lane = iota((count, ATOMS), 1)
        spread = onehot_of(lane == centre)
        named = dot_nt(spread, cells_ref[...]) * 8.0 + dot_nt(spread, within_ref[...])
        named = select_lane(named, edge % HALF, 0.0)
        live_count = jnp.sum(jnp.where(lane == centre, counts_ref[...].astype(F32), 0.0), axis=1, keepdims=True)
        hit = lane.astype(F32) == named
        edge_pair = jnp.where(hit, 1.0, jnp.where(lane == centre, -1.0, 0.0)).astype(BF16)
        pair_ref[rows, :] = edge_pair
        relt_ref[:, rows] = gather_places(edge_pair, parts, True)
        hot_ref[rows, :] = onehot_of(jnp.logical_and(hit, (edge % HALF).astype(F32) < live_count))
        radial_of(gather_places(edge_pair, parts, False), rbf_ref, radial_ref, rad_ref, drad_ref, rows)

    for start in range(0, ATOMS * HALF, HEAD):
        geometry(start, HEAD)
    advance(1)

    @pl.loop(0, OWN_CHUNKS)
    def _(chunk):
        here = pl.ds(pl.multiple_of(chunk * atoms, atoms), atoms)
        rows = pl.ds(pl.multiple_of(chunk * OWN_ROWS, OWN_ROWS), OWN_ROWS)
        onehot = hot_ref[rows, :]

        def put_slope(lanes, value):
            slope_ref[rows, lanes] = value

        def middle():
            for at, step in ((1, 3), (2, 4)):
                @pl.when(chunk == at)
                def _():
                    advance(step)

        edge_forward(onehot, feat_ref, rad_ref, drad_ref, rows, block_ref, mix_ref, lhs_ref, message_ref, put_slope, middle=middle)
        for pair in PAIRS:
            lanes = slice(pair[0] * C, (pair[-1] + 1) * C)
            acc_ref[here, lanes] = dot(gather, message_ref[:, lanes])
        copy_out(chunk).start()

        for at, steps in ((0, (2,)), (3, (5,))):
            @pl.when(chunk == at)
            def _():
                for step in steps:
                    advance(step)

    advance(6)
    for copy in plan.values():
        copy.wait_send()
    for chunk in range(OWN_CHUNKS):
        copy_out(chunk).wait()


def own_edges(*operands):
    vmem = pl.BlockSpec(memory_space=pltpu.VMEM)
    edges = ATOMS * HALF
    return pl.pallas_call(
        own_body,
        out_shape=(
            jax.ShapeDtypeStruct((ATOMS, FEAT), F32),
            jax.ShapeDtypeStruct((8, edges), F32),
            jax.ShapeDtypeStruct((edges, ATOMS), BF16),
            jax.ShapeDtypeStruct((4, 4, 4, 8, WIDE), BF16),
            jax.ShapeDtypeStruct((len(BLOCKS), 2 * C, 2 * C), BF16),
            jax.ShapeDtypeStruct((len(BLOCKS), 2 * C, 2 * C), BF16),
            jax.ShapeDtypeStruct((edges, FEAT), BF16),
        ),
        in_specs=[pl.BlockSpec(memory_space=pltpu.HBM)] * len(operands),
        out_specs=(vmem,) * 6 + (pl.BlockSpec(memory_space=pl.ANY),),
        scratch_shapes=like(operands)
        + [
            pltpu.VMEM((8, ATOMS), F32),
            pltpu.VMEM((SLOTS, ATOMS), BF16),
            pltpu.VMEM((SLOTS, ATOMS), BF16),
            pltpu.VMEM((edges, DEGREES * C), BF16),
            pltpu.VMEM((edges, DEGREES * C), BF16),
            pltpu.VMEM((edges, ATOMS), BF16),
            pltpu.VMEM((2 * OWN_ROWS, FEAT), BF16),
            pltpu.VMEM((OWN_ROWS, FEAT), BF16),
            pltpu.VMEM((edges, FEAT), BF16),
            pltpu.SemaphoreType.DMA((OWN_CHUNKS,)),
            pltpu.SemaphoreType.DMA((HALO_COPIES,)),
            pltpu.SemaphoreType.DMA((HALO_COPIES,)),
        ],
        compiler_params=pltpu.CompilerParams(vmem_limit_bytes=VMEM_LIMIT, collective_id=0, has_side_effects=True),
        cost_estimate=pl.CostEstimate(flops=8_000_000_000, bytes_accessed=10_000_000, transcendentals=600_000),
        name="own_edges",
    )(*operands)


def ghost_body(
    feat_hbm, pos_hbm, neigh_hbm, counts_hbm, rbf_hbm, radial_hbm, mix_hbm, out_hbm,
    energy_hbm, norm_hbm, acc_own_ref, relt_ref, pair_ref, table_ref, block_ref, oblock_ref, slope_hbm,
    new_ref, energies_ref, grad_own_ref, tiles_ref,
    feat_ref, pos_ref, neigh_ref, counts_ref, rbf_ref, radial_ref, mix_ref, out_ref,
    energy_ref, norm_ref, load_sem,
    pos8_ref, cells_ref, within_ref, rad_ref, drad_ref, lhs_ref, message_ref,
    slope_ref, gslope_ref, acc_ref, grelt_ref, gslot_ref, gatom_ref, hot_ref, last_ref, updated_ref, grad_ref, gsum_ref, sem,
):
    loads = load_all(
        (pos_hbm, neigh_hbm, counts_hbm, rbf_hbm, radial_hbm, mix_hbm, out_hbm, feat_hbm, energy_hbm, norm_hbm),
        (pos_ref, neigh_ref, counts_ref, rbf_ref, radial_ref, mix_ref, out_ref, feat_ref, energy_ref, norm_ref),
        load_sem,
    )
    load_slope = pltpu.make_async_copy(slope_hbm, slope_ref, sem)
    load_slope.start()
    for at in (0, 1, 2):
        loads[at].wait()
    pos8_ref[...] = jnp.zeros(pos8_ref.shape, F32)
    pos8_ref[0:3, :] = pos_ref[:, 0, :]
    stacked = [part.astype(F32) for part in split3(pos8_ref[...])] + [jnp.zeros((C - 24, ATOMS), F32)]
    stacked = jnp.concatenate(stacked, axis=0).astype(BF16)
    cells, within = neighbour_parts(neigh_ref)
    cells_ref[...] = cells
    within_ref[...] = within
    live_row = jnp.maximum(counts_ref[...].astype(F32) - float(HALF), 0.0)
    square = (ATOMS, ATOMS)
    row_id, col_id = iota(square, 0), iota(square, 1)
    live_col = jnp.sum(jnp.where(row_id == col_id, live_row, 0.0), axis=1, keepdims=True)
    start_col = jnp.sum(jnp.where(col_id < row_id, live_row, 0.0), axis=1, keepdims=True)
    start_row = jnp.sum(jnp.where(row_id < col_id, live_col, 0.0), axis=0, keepdims=True)
    total = jnp.sum(live_row).astype(jnp.int32)
    chunks = (total + GHOST_ROWS - 1) // GHOST_ROWS
    acc_ref[...] = acc_own_ref[...]
    for copy in loads[3:]:
        copy.wait()

    def whole(gathered):
        return gathered + (pltpu.roll(gathered, C - 8, 1) + pltpu.roll(gathered, C - 16, 1))

    def spread_of(start, count):
        place = (iota((ATOMS, count), 1) + start).astype(F32)
        return jnp.logical_and(place >= start_col, place < start_col + live_col)

    def geometry(start, count):
        rows = pl.ds(start, count)
        place = (iota((count, 1), 0) + start).astype(F32)
        inside = jnp.logical_and(place >= start_row, place < start_row + live_row)
        begin = jnp.sum(jnp.where(inside, start_row, 0.0), axis=1, keepdims=True)
        spread = onehot_of(inside)
        named = dot_nt(spread, cells_ref[...]) * 8.0 + dot_nt(spread, within_ref[...])
        named = select_lane(named, (place - begin).astype(jnp.int32) + HALF, 0.0)
        onehot = onehot_of(iota((count, GHOST), 1).astype(F32) == named - float(ATOMS))
        row = named.astype(jnp.int32) - ATOMS
        inside = row >= 0
        row = jnp.maximum(row, 0)
        spots = [(row >> shift) & 3 for shift in (7, 5, 3)]
        moves = [jnp.where(spot == 0, -1, jnp.where(spot == 3, 1, 0)) for spot in spots]
        toward = moves[0] * 9 + moves[1] * 3 + moves[2] + 13
        slot = row & 7
        for at, spot in enumerate(spots):
            slot = slot + (((spot + 1) & 1) << (5 - at))
        place = jnp.where(inside, toward * ATOMS + slot, -1)
        hot_ref[rows, :] = onehot
        gslot_ref[rows, :] = onehot_of(iota((count, TILES * C), 1) == place)
        gatom_ref[rows, :] = spread
        lane = iota((count, C), 1)
        last = dot(onehot, table_ref[:, FEAT - C :])
        image = jnp.zeros((count, C), F32)
        for at, move in enumerate(moves):
            image = jnp.where(lane == at, move.astype(F32) * 4.0, image)
        rel = (whole(last[:, C:]) + image) - whole(dot_nt(spread, stacked))
        rel = jnp.where(jnp.logical_and(lane < 3, inside), rel, 0.0)
        grelt_ref[:, rows] = rel.T[:8]
        last_ref[rows, :] = last[:, :C].astype(BF16)
        radial_of(rel, rbf_ref, radial_ref, rad_ref, drad_ref, rows)

    tails = jnp.maximum(total - HEAD + TAIL - 1, 0) // TAIL
    tail_at = lambda at: pl.multiple_of(HEAD + at * TAIL, TAIL)
    geometry(0, HEAD)

    @pl.loop(0, tails)
    def _(at):
        geometry(tail_at(at), TAIL)

    @pl.loop(0, chunks)
    def _(chunk):
        rows = pl.ds(pl.multiple_of(chunk * GHOST_ROWS, GHOST_ROWS), GHOST_ROWS)

        def put_slope(lanes, value):
            gslope_ref[rows, lanes] = value

        onehot, last = hot_ref[rows, :], last_ref[rows, :]
        gather = onehot_of(spread_of(chunk * GHOST_ROWS, GHOST_ROWS))
        edge_forward(onehot, table_ref, rad_ref, drad_ref, rows, block_ref, mix_ref, lhs_ref, message_ref, put_slope, last)
        for pair in PAIRS:
            lanes = slice(pair[0] * C, (pair[-1] + 1) * C)
            acc_ref[:, lanes] += dot(gather, message_ref[:, lanes])

    for pair in PAIRS:
        lanes = slice(pair[0] * C, (pair[-1] + 1) * C)
        low = (acc_ref[:, lanes] * NORM).astype(BF16)
        updated_ref[:, lanes] = dot(low, pair_weight(pair, oblock_ref, out_ref))
    energy = None
    for k in range(COEFFS):
        lanes = slice(k * C, (k + 1) * C)
        value = feat_ref[:, lanes].astype(F32) + updated_ref[:, lanes]
        new_ref[:, lanes] = value.astype(BF16)
        if k == 0:
            logistic = jax.nn.sigmoid(value)
            scale = energy_ref[...]
            term = scale * value * logistic
            grad = scale * logistic * (1.0 + value * (1.0 - logistic))
        else:
            degree = DEGREE[k]
            scaled = norm_ref[degree - 1 : degree, :] * (1.0 / (2 * degree + 1)) * value
            term = scaled * value
            grad = 2.0 * scaled
        energy = term if energy is None else energy + term
        grad_ref[:, lanes] = grad.astype(BF16)
    for pair in PAIRS:
        lanes = slice(pair[0] * C, (pair[-1] + 1) * C)
        weight = pair_weight(pair, oblock_ref, out_ref)
        gsum_ref[lanes, :] = (dot_nt(weight, grad_ref[:, lanes]) * NORM).astype(BF16)
    energy = jnp.sum(energy, axis=1, keepdims=True)
    energies_ref[...] = jnp.sum(jnp.where(row_id == col_id, energy, 0.0), axis=0, keepdims=True)

    def pull_of(relt, slope_grad):
        square = jnp.sum(relt * relt, axis=0, keepdims=True)
        pull = relt * (slope_grad * jnp.where(square > 0.0, lax.rsqrt(square), 0.0))
        high = pull.astype(BF16)
        return jnp.concatenate([high, (pull - high.astype(F32)).astype(BF16)], axis=0)

    load_slope.wait()

    own_total = jnp.zeros((16, ATOMS), F32)
    for start in range(0, ATOMS * HALF, OWN_ROWS):
        rows = slice(start, start + OWN_ROWS)
        slopes = dot(slope_ref[rows, :], gsum_ref[...]).T
        own = (iota((ATOMS, OWN_ROWS), 1) + start) // HALF == iota((ATOMS, OWN_ROWS), 0)
        slopes = jnp.sum(jnp.where(own, slopes, 0.0), axis=0, keepdims=True)
        own_total = own_total + dot(pull_of(relt_ref[:, rows], slopes), pair_ref[rows, :])

    def ghost_step(start, count, totals):
        own_total, ghost_total = totals
        rows = pl.ds(start, count)
        slopes = dot(gslope_ref[rows, :], gsum_ref[...]).T
        slopes = jnp.sum(jnp.where(spread_of(start, count), slopes, 0.0), axis=0, keepdims=True)
        pull = pull_of(grelt_ref[:, rows], slopes)
        return own_total - dot(pull, gatom_ref[rows, :]), ghost_total + dot(pull, gslot_ref[rows, :])

    totals = ghost_step(0, HEAD, (own_total, jnp.zeros((16, TILES * C), F32)))
    own_total, ghost_total = lax.fori_loop(0, tails, lambda at, total: ghost_step(tail_at(at), TAIL, total), totals)
    grad_own_ref[...] = own_total[:8] + own_total[8:]
    for tile in range(TILES):
        lanes = slice(tile * C, (tile + 1) * C)
        tiles_ref[tile] = ghost_total[:8, lanes] + ghost_total[8:, lanes]


def ghost_edges(*operands):
    vmem = pl.BlockSpec(memory_space=pltpu.VMEM)
    hbm = pl.BlockSpec(memory_space=pl.ANY)
    own = ATOMS * HALF
    return pl.pallas_call(
        ghost_body,
        out_shape=(
            jax.ShapeDtypeStruct((ATOMS, FEAT), BF16),
            jax.ShapeDtypeStruct((1, ATOMS), F32),
            jax.ShapeDtypeStruct((8, ATOMS), F32),
            jax.ShapeDtypeStruct((TILES, 8, C), F32),
        ),
        in_specs=[pl.BlockSpec(memory_space=pltpu.HBM)] * 10 + [vmem] * 6 + [hbm],
        out_specs=(vmem,) * 4,
        scratch_shapes=like(operands[:10])
        + [
            pltpu.VMEM((8, ATOMS), F32),
            pltpu.VMEM((SLOTS, ATOMS), BF16),
            pltpu.VMEM((SLOTS, ATOMS), BF16),
            pltpu.VMEM((GHOST_EDGES, DEGREES * C), BF16),
            pltpu.VMEM((GHOST_EDGES, DEGREES * C), BF16),
            pltpu.VMEM((2 * GHOST_ROWS, FEAT), BF16),
            pltpu.VMEM((GHOST_ROWS, FEAT), BF16),
            pltpu.VMEM((own, FEAT), BF16),
            pltpu.VMEM((GHOST_EDGES, FEAT), BF16),
            pltpu.VMEM((ATOMS, FEAT), F32),
            pltpu.VMEM((8, GHOST_EDGES), F32),
            pltpu.VMEM((GHOST_EDGES, TILES * C), BF16),
            pltpu.VMEM((GHOST_EDGES, ATOMS), BF16),
            pltpu.VMEM((GHOST_EDGES, GHOST), BF16),
            pltpu.VMEM((GHOST_EDGES, C), BF16),
            pltpu.VMEM((ATOMS, FEAT), F32),
            pltpu.VMEM((ATOMS, FEAT), BF16),
            pltpu.VMEM((FEAT, ATOMS), BF16),
            pltpu.SemaphoreType.DMA,
        ],
        compiler_params=pltpu.CompilerParams(vmem_limit_bytes=VMEM_LIMIT),
        cost_estimate=pl.CostEstimate(flops=10_000_000_000, bytes_accessed=14_000_000, transcendentals=400_000),
        name="ghost_edges",
    )(*operands)


def return_body(tiles_ref, grad_own_ref, order_hbm, forces_ref, order_ref, load_sem, landed_ref, send_sem, recv_sem):
    loads = load_all((order_hbm,), (order_ref,), load_sem)
    here = [lax.axis_index(axis) for axis in ("gx", "gy", "gz")]
    sizes = [lax.axis_size(axis) for axis in ("gx", "gy", "gz")]
    barrier = pltpu.get_barrier_semaphore()
    others = [at for at in range(DIRECTIONS) if at != DIRECTIONS // 2]
    copies = []
    for at in others:
        moves = (at // 9 - 1, at // 3 % 3 - 1, at % 3 - 1)
        device = tuple(lax.rem(h + n + m, n) for h, n, m in zip(here, sizes, moves))
        pl.semaphore_signal(barrier, inc=1, device_id=device, device_id_type=MESH_ID)
        copies.append(
            pltpu.make_async_remote_copy(
                src_ref=tiles_ref.at[at // 2], dst_ref=landed_ref.at[at],
                send_sem=send_sem.at[at], recv_sem=recv_sem.at[at],
                device_id=device, device_id_type=MESH_ID,
            )
        )
    pl.semaphore_wait(barrier, len(others))
    for copy in copies:
        copy.start()
    loads[0].wait()
    listed = column_of(order_ref[...].astype(F32)) == iota((ATOMS, ATOMS), 1).astype(F32)
    listed = onehot_of(listed)
    for copy in copies:
        copy.wait_recv()
    even = sum(landed_ref[at] for at in others if at % 2 == 0)
    odd = sum(landed_ref[at] for at in others if at % 2 == 1)
    total = (even + pltpu.roll(odd, ATOMS, 1))[:, :ATOMS]
    back = sum(dot(part, listed) for part in split3(total)[::-1])
    forces_ref[:, 0, :] = -(grad_own_ref[...] + back)[:3]
    for copy in copies:
        copy.wait_send()


def return_forces(tiles, grad_own, order):
    vmem = pl.BlockSpec(memory_space=pltpu.VMEM)
    return pl.pallas_call(
        return_body,
        out_shape=jax.ShapeDtypeStruct((3, 1, ATOMS), F32),
        in_specs=[vmem] * 2 + [pl.BlockSpec(memory_space=pltpu.HBM)],
        out_specs=vmem,
        scratch_shapes=like((order,))
        + [
            pltpu.VMEM((DIRECTIONS, 8, C), F32),
            pltpu.SemaphoreType.DMA((DIRECTIONS,)),
            pltpu.SemaphoreType.DMA((DIRECTIONS,)),
        ],
        compiler_params=pltpu.CompilerParams(collective_id=1, has_side_effects=True, vmem_limit_bytes=4 * 1024 * 1024),
        name="return_forces",
    )(tiles, grad_own, order)


def local(
    features, positions, neighbours, counts, cell_atoms,
    rbf_weight, radial_weight, mix_weight, out_weight, energy_weight, norm_weight,
):
    feat = features.reshape(ATOMS, FEAT)
    pos = positions.reshape(3, 1, ATOMS)
    neigh = jnp.transpose(neighbours.reshape(ATOMS, SLOTS))
    live = counts.reshape(1, ATOMS)
    order = cell_atoms.reshape(1, ATOMS)
    energy, norm = energy_weight.reshape(1, C), norm_weight
    feat, pos, neigh, live, order, rbf_weight, radial_weight, mix_weight, out_weight, energy, norm = (
        pltpu.with_memory_space_constraint(operand, pltpu.HBM)
        for operand in (feat, pos, neigh, live, order, rbf_weight, radial_weight, mix_weight, out_weight, energy, norm)
    )
    acc, relt, pairs, table, blocks, oblocks, slopes = own_edges(
        feat, pos, neigh, live, order, rbf_weight, radial_weight, mix_weight, out_weight
    )
    updated, energies, grad_own, tiles = ghost_edges(
        feat, pos, neigh, live, rbf_weight, radial_weight, mix_weight, out_weight,
        energy, norm, acc, relt, pairs, table.reshape(GHOST, WIDE), blocks, oblocks, slopes,
    )
    forces = return_forces(tiles, grad_own, order)
    return (
        updated.reshape(features.shape),
        energies.reshape(counts.shape),
        forces.reshape(positions.shape),
    )


def solution(mesh):
    spread = P("gx", "gy", "gz", None, None)
    rows = P("gx", "gy", "gz", None)
    return jax.shard_map(
        local,
        mesh=mesh,
        in_specs=(spread, spread, spread, rows, rows) + (P(),) * 6,
        out_specs=(spread, rows, spread),
        check_vma=False,
    )
```

```python
import math

import jax
import jax.numpy as jnp
from jax import lax
from jax.experimental import pallas as pl
from jax.experimental.pallas import tpu as pltpu
from jax.sharding import PartitionSpec as P

F32, BF16 = jnp.float32, jnp.bfloat16
ATOMS, SLOTS, HALF, C, FEAT, RBF, DEGREES = 64, 32, 16, 128, 3200, 512, 5
GHOST = 512
WIDE = FEAT + C
DIRECTIONS = 27
TILES = 14
MESH_ID = pl.DeviceIdType.MESH
COEFFS = FEAT // C
DEGREE = [degree for degree in range(DEGREES) for _ in range(2 * degree + 1)]
PAIRS = [tuple(range(k, min(k + 2, COEFFS))) for k in range(0, COEFFS, 2)]
BLOCKS = sorted({(DEGREE[a], DEGREE[b]) for a, b in PAIRS[:-1]})
NORM = 1.0 / math.sqrt(SLOTS)
SPACING = 2.0 * math.sqrt(48.0) / (RBF - 1)
OWN_ROWS = 256
OWN_CHUNKS = ATOMS * HALF // OWN_ROWS
GHOST_ROWS = 256
HEAD = 512
TAIL = 256
GHOST_EDGES = ATOMS * HALF
VMEM_LIMIT = 40 * 1024 * 1024


def dot(a, b):
    return lax.dot_general(a, b, (((1,), (0,)), ((), ())), preferred_element_type=F32)


def dot_nt(a, b):
    return lax.dot_general(a, b, (((1,), (1,)), ((), ())), preferred_element_type=F32)


def iota(shape, dim):
    return lax.broadcasted_iota(jnp.int32, shape, dim)


def onehot_of(hit):
    return jnp.where(hit, 1.0, 0.0).astype(BF16)


def split3(value):
    high = value.astype(BF16)
    rest = value - high.astype(F32)
    middle = rest.astype(BF16)
    return high, middle, (rest - middle.astype(F32)).astype(BF16)


def gather_places(onehot, parts, flipped):
    total = None
    for part in parts[::-1]:
        value = dot_nt(part, onehot) if flipped else dot_nt(onehot, part)
        total = value if total is None else total + value
    return total


def fill_blocks(block_ref, weight_ref):
    block_ref[...] = jnp.zeros(block_ref.shape, BF16)
    for at, (first, second) in enumerate(BLOCKS):
        block_ref[at, :C, :C] = weight_ref[first]
        block_ref[at, C:, C:] = weight_ref[second]


def pair_weight(pair, block_ref, weight_ref):
    if len(pair) == 1:
        return weight_ref[DEGREE[pair[0]]]
    return block_ref[BLOCKS.index((DEGREE[pair[0]], DEGREE[pair[1]]))]


def wide(value, pair):
    return value if len(pair) == 1 else jnp.concatenate([value, value], axis=1)


def radial_of(rel, rbf_ref, radial_ref, rad_ref, drad_ref, at):
    distance = jnp.sqrt(jnp.sum(rel * rel, axis=1, keepdims=True))
    rows = rel.shape[0]
    centred = distance * (1.0 / SPACING) - iota((rows, RBF), 1).astype(F32)
    basis = jnp.exp(-0.5 * centred * centred)
    preact = dot(basis.astype(BF16), rbf_ref[...])
    slope = dot((basis * centred).astype(BF16), rbf_ref[...]) * (-1.0 / SPACING)
    logistic = jax.nn.sigmoid(preact)
    hidden = (preact * logistic).astype(BF16)
    dhidden = (slope * logistic * (1.0 + preact * (1.0 - logistic))).astype(BF16)
    rad_ref[at, :] = dot(hidden, radial_ref[...]).astype(BF16)
    drad_ref[at, :] = dot(dhidden, radial_ref[...]).astype(BF16)


def edge_forward(onehot, table_ref, rad_ref, drad_ref, at_rows, block_ref, mix_ref, lhs_ref, message_ref, put_slope, last=None, middle=None):
    rows = onehot.shape[0]
    for pair in PAIRS:
        lanes = slice(pair[0] * C, (pair[-1] + 1) * C)
        if len(pair) == 1 and last is not None:
            near = last
        else:
            near = dot(onehot, table_ref[:, lanes]).astype(BF16)
        for at, k in enumerate(pair):
            cut = slice(DEGREE[k] * C, (DEGREE[k] + 1) * C)
            half = near[:, at * C : (at + 1) * C]
            lhs_ref[:rows, k * C : (k + 1) * C] = half * rad_ref[at_rows, cut]
            lhs_ref[rows:, k * C : (k + 1) * C] = half * drad_ref[at_rows, cut]
    if middle is not None:
        middle()
    gate = lean = None
    for pair in PAIRS:
        lanes = slice(pair[0] * C, (pair[-1] + 1) * C)
        both = dot(lhs_ref[:, lanes], pair_weight(pair, block_ref, mix_ref))
        mixed, dmixed = both[:rows], both[rows:]
        if gate is None:
            gate = jax.nn.sigmoid(mixed[:, :C])
            lean = (1.0 - gate) * dmixed[:, :C]
        message_ref[:, lanes] = (mixed * wide(gate, pair)).astype(BF16)
        put_slope(lanes, ((dmixed + mixed * wide(lean, pair)) * wide(gate, pair)).astype(BF16))


def select_lane(table, lane, value):
    return jnp.sum(jnp.where(iota(table.shape, 1) == lane, table, 0.0), axis=1, keepdims=True)


def neighbour_parts(neigh_ref):
    rows = neigh_ref[...]
    return (rows >> 3).astype(F32).astype(BF16), (rows & 7).astype(F32).astype(BF16)


def column_of(row):
    square = (ATOMS, ATOMS)
    return jnp.sum(jnp.where(iota(square, 0) == iota(square, 1), row, 0.0), axis=1, keepdims=True)


def halo_copies(table_ref, send_sem, recv_sem):
    gx, gy, gz = (lax.axis_index(axis) for axis in ("gx", "gy", "gz"))
    nx, ny, nz = (lax.axis_size(axis) for axis in ("gx", "gy", "gz"))
    odd = lax.rem(gx, 2)
    sibling = (gx + 1 - 2 * odd, gy, gz)
    far = (lax.rem(gx + nx - 1 + 2 * odd, nx), gy, gz)
    down_y, up_y = ((gx, lax.rem(gy + ny + step, ny), gz) for step in (-1, 1))
    down_z, up_z = ((gx, gy, lax.rem(gz + nz + step, nz)) for step in (-1, 1))
    far_cell, shared, far_own = 3 * odd, 2 - odd, 1 + odd
    far_target, sibling_target = 3 - 3 * odd, 3 * odd
    one = lambda at: pl.ds(at, 1)
    inner, whole = pl.ds(1, 2), pl.ds(0, 4)
    plan = {}

    def add(name, device, x, y, z, to_x=None, to_y=None, to_z=None):
        at = len(plan)
        source = table_ref.at[x, y, z]
        target = table_ref.at[
            x if to_x is None else one(to_x), y if to_y is None else one(to_y), z if to_z is None else one(to_z)
        ]
        plan[name] = pltpu.make_async_remote_copy(
            src_ref=source, dst_ref=target, send_sem=send_sem.at[at], recv_sem=recv_sem.at[at],
            device_id=device, device_id_type=MESH_ID,
        )

    add("far", far, one(far_own), inner, inner, to_x=far_target)
    for x, kind in ((inner, "own"), (one(far_cell), "far")):
        add(kind + "_yd_a", down_y, x, one(1), one(1), to_y=3)
        add(kind + "_yu_a", up_y, x, one(2), one(2), to_y=0)
        add(kind + "_zd_a", down_z, x, one(2), one(1), to_z=3)
        add(kind + "_zu_a", up_z, x, one(1), one(2), to_z=0)
        add(kind + "_yd_b", down_y, x, one(1), one(2), to_y=3)
        add(kind + "_yu_b", up_y, x, one(2), one(1), to_y=0)
        add(kind + "_zd_b", down_z, x, one(1), one(1), to_z=3)
        add(kind + "_zu_b", up_z, x, one(2), one(2), to_z=0)
        add(kind + "_zd_e", down_z, x, one(3), one(1), to_z=3)
        add(kind + "_zu_e", up_z, x, one(0), one(2), to_z=0)
        add(kind + "_yd_e", down_y, x, one(1), one(0), to_y=3)
        add(kind + "_yu_e", up_y, x, one(2), one(3), to_y=0)
    add("sib", sibling, one(shared), inner, inner, to_x=sibling_target)
    for edge in (0, 3):
        add("sib_y%d" % edge, sibling, one(shared), one(edge), inner, to_x=sibling_target)
        add("sib_z%d" % edge, sibling, one(shared), inner, one(edge), to_x=sibling_target)
        add("sib_e%d0" % edge, sibling, one(shared), one(edge), one(0), to_x=sibling_target)
        add("sib_e%d3" % edge, sibling, one(shared), one(edge), one(3), to_x=sibling_target)
    return plan, (sibling, far, down_y, up_y, down_z, up_z)


def halo_steps(plan):
    sides = ("_yd", "_yu", "_zd", "_zu")
    names = lambda kind, piece: [kind + side + piece for side in sides]
    steps = (
        ([], ["far"] + names("own", "_a") + names("own", "_b") + ["sib"]),
        (names("own", "_a"), names("own", "_e")),
        (["far"], names("far", "_a") + names("far", "_b")),
        (names("own", "_b"), ["sib_y0", "sib_y3", "sib_z0", "sib_z3"]),
        (names("far", "_a"), names("far", "_e")),
        (names("own", "_e"), ["sib_e00", "sib_e03", "sib_e30", "sib_e33"]),
        (names("far", "_b") + names("far", "_e") + [name for name in plan if name.startswith("sib")], []),
    )

    def run(step):
        for name in steps[step][0]:
            plan[name].wait_recv()
        for name in steps[step][1]:
            plan[name].start()

    return run


HALO_COPIES = 34


def load_all(sources, targets, sem):
    copies = [pltpu.make_async_copy(a, b, sem.at[at]) for at, (a, b) in enumerate(zip(sources, targets))]
    for copy in copies:
        copy.start()
    return copies


def like(operands):
    return [pltpu.VMEM(operand.shape, operand.dtype) for operand in operands] + [
        pltpu.SemaphoreType.DMA((len(operands),))
    ]


def own_body(
    feat_hbm, pos_hbm, neigh_hbm, counts_hbm, order_hbm, rbf_hbm, radial_hbm, mix_hbm, out_hbm,
    feat_ref, pos_ref, neigh_ref, counts_ref, order_ref, rbf_ref, radial_ref, mix_ref, out_ref,
    acc_ref, relt_ref, pair_ref, table_ref, block_ref, oblock_ref, slope_hbm,
    load_sem,
    pos8_ref, cells_ref, within_ref, rad_ref, drad_ref, hot_ref, lhs_ref, message_ref, slope_ref, sem, send_sem, recv_sem,
):
    loads = load_all(
        (feat_hbm, pos_hbm, neigh_hbm, counts_hbm, order_hbm, rbf_hbm, radial_hbm, mix_hbm, out_hbm),
        (feat_ref, pos_ref, neigh_ref, counts_ref, order_ref, rbf_ref, radial_ref, mix_ref, out_ref),
        load_sem,
    )
    plan, devices = halo_copies(table_ref, send_sem, recv_sem)
    barrier = pltpu.get_barrier_semaphore()
    for device in devices:
        pl.semaphore_signal(barrier, inc=1, device_id=device, device_id_type=MESH_ID)
    pos8_ref[...] = jnp.zeros(pos8_ref.shape, F32)
    for at in (0, 1, 4):
        loads[at].wait()
    pos8_ref[0:3, :] = pos_ref[:, 0, :]
    parts = split3(pos8_ref[...])
    listed = column_of(order_ref[...].astype(F32)) == iota((ATOMS, ATOMS), 1).astype(F32)
    listed = onehot_of(listed)
    box = (2, 2, 2, 8)
    for start in range(0, FEAT, 2 * C):
        lanes = slice(start, min(start + 2 * C, FEAT))
        value = dot(listed, feat_ref[:, lanes])
        table_ref[1:3, 1:3, 1:3, :, lanes] = value.reshape(box + (value.shape[1],)).astype(BF16)
    stacked = [part.astype(F32) for part in parts] + [jnp.zeros((C - 24, ATOMS), F32)]
    value = dot_nt(listed, jnp.concatenate(stacked, axis=0).astype(BF16))
    table_ref[1:3, 1:3, 1:3, :, FEAT:] = value.reshape(box + (C,)).astype(BF16)
    for at in (7, 8):
        loads[at].wait()
    fill_blocks(block_ref, mix_ref)
    fill_blocks(oblock_ref, out_ref)
    advance = halo_steps(plan)
    pl.semaphore_wait(barrier, len(devices))
    advance(0)
    for at in (2, 3, 5, 6):
        loads[at].wait()
    cells, within = neighbour_parts(neigh_ref)
    cells_ref[...] = cells
    within_ref[...] = within
    atoms = OWN_ROWS // HALF
    gather = onehot_of(iota((atoms, OWN_ROWS), 1) // HALF == iota((atoms, OWN_ROWS), 0))

    def copy_out(chunk):
        return pltpu.make_async_copy(
            slope_ref.at[pl.ds(chunk * OWN_ROWS, OWN_ROWS), :],
            slope_hbm.at[pl.ds(chunk * OWN_ROWS, OWN_ROWS), :],
            sem.at[chunk],
        )

    def geometry(start, count):
        rows = slice(start, start + count)
        edge = iota((count, 1), 0)
        centre = (start + edge) // HALF
        lane = iota((count, ATOMS), 1)
        spread = onehot_of(lane == centre)
        named = dot_nt(spread, cells_ref[...]) * 8.0 + dot_nt(spread, within_ref[...])
        named = select_lane(named, edge % HALF, 0.0)
        live_count = jnp.sum(jnp.where(lane == centre, counts_ref[...].astype(F32), 0.0), axis=1, keepdims=True)
        hit = lane.astype(F32) == named
        edge_pair = jnp.where(hit, 1.0, jnp.where(lane == centre, -1.0, 0.0)).astype(BF16)
        pair_ref[rows, :] = edge_pair
        relt_ref[:, rows] = gather_places(edge_pair, parts, True)
        hot_ref[rows, :] = onehot_of(jnp.logical_and(hit, (edge % HALF).astype(F32) < live_count))
        radial_of(gather_places(edge_pair, parts, False), rbf_ref, radial_ref, rad_ref, drad_ref, rows)

    for start in range(0, ATOMS * HALF, HEAD):
        geometry(start, HEAD)
    advance(1)

    @pl.loop(0, OWN_CHUNKS)
    def _(chunk):
        here = pl.ds(pl.multiple_of(chunk * atoms, atoms), atoms)
        rows = pl.ds(pl.multiple_of(chunk * OWN_ROWS, OWN_ROWS), OWN_ROWS)
        onehot = hot_ref[rows, :]

        def put_slope(lanes, value):
            slope_ref[rows, lanes] = value

        def middle():
            for at, step in ((1, 3), (2, 4)):
                @pl.when(chunk == at)
                def _():
                    advance(step)

        edge_forward(onehot, feat_ref, rad_ref, drad_ref, rows, block_ref, mix_ref, lhs_ref, message_ref, put_slope, middle=middle)
        for pair in PAIRS:
            lanes = slice(pair[0] * C, (pair[-1] + 1) * C)
            acc_ref[here, lanes] = dot(gather, message_ref[:, lanes])
        copy_out(chunk).start()

        for at, steps in ((0, (2,)), (3, (5,))):
            @pl.when(chunk == at)
            def _():
                for step in steps:
                    advance(step)

    advance(6)
    for copy in plan.values():
        copy.wait_send()
    for chunk in range(OWN_CHUNKS):
        copy_out(chunk).wait()


def own_edges(*operands):
    vmem = pl.BlockSpec(memory_space=pltpu.VMEM)
    edges = ATOMS * HALF
    return pl.pallas_call(
        own_body,
        out_shape=tuple(jax.ShapeDtypeStruct(operand.shape, operand.dtype) for operand in operands)
        + (
            jax.ShapeDtypeStruct((ATOMS, FEAT), F32),
            jax.ShapeDtypeStruct((8, edges), F32),
            jax.ShapeDtypeStruct((edges, ATOMS), BF16),
            jax.ShapeDtypeStruct((4, 4, 4, 8, WIDE), BF16),
            jax.ShapeDtypeStruct((len(BLOCKS), 2 * C, 2 * C), BF16),
            jax.ShapeDtypeStruct((len(BLOCKS), 2 * C, 2 * C), BF16),
            jax.ShapeDtypeStruct((edges, FEAT), BF16),
        ),
        in_specs=[pl.BlockSpec(memory_space=pltpu.HBM)] * len(operands),
        out_specs=(vmem,) * (6 + len(operands)) + (pl.BlockSpec(memory_space=pl.ANY),),
        scratch_shapes=[
            pltpu.SemaphoreType.DMA((len(operands),)),
            pltpu.VMEM((8, ATOMS), F32),
            pltpu.VMEM((SLOTS, ATOMS), BF16),
            pltpu.VMEM((SLOTS, ATOMS), BF16),
            pltpu.VMEM((edges, DEGREES * C), BF16),
            pltpu.VMEM((edges, DEGREES * C), BF16),
            pltpu.VMEM((edges, ATOMS), BF16),
            pltpu.VMEM((2 * OWN_ROWS, FEAT), BF16),
            pltpu.VMEM((OWN_ROWS, FEAT), BF16),
            pltpu.VMEM((edges, FEAT), BF16),
            pltpu.SemaphoreType.DMA((OWN_CHUNKS,)),
            pltpu.SemaphoreType.DMA((HALO_COPIES,)),
            pltpu.SemaphoreType.DMA((HALO_COPIES,)),
        ],
        compiler_params=pltpu.CompilerParams(vmem_limit_bytes=VMEM_LIMIT, collective_id=0, has_side_effects=True),
        cost_estimate=pl.CostEstimate(flops=8_000_000_000, bytes_accessed=10_000_000, transcendentals=600_000),
        name="own_edges",
    )(*operands)


def ghost_body(
    energy_hbm, norm_hbm, feat_ref, pos_ref, neigh_ref, counts_ref, rbf_ref, radial_ref, mix_ref, out_ref,
    acc_own_ref, relt_ref, pair_ref, table_ref, block_ref, oblock_ref, slope_hbm,
    new_ref, energies_ref, grad_own_ref, tiles_ref,
    energy_ref, norm_ref, load_sem,
    pos8_ref, cells_ref, within_ref, rad_ref, drad_ref, lhs_ref, message_ref,
    slope_ref, gslope_ref, acc_ref, grelt_ref, gslot_ref, gatom_ref, hot_ref, last_ref, updated_ref, grad_ref, gsum_ref, sem,
):
    loads = load_all(
        (energy_hbm, norm_hbm),
        (energy_ref, norm_ref),
        load_sem,
    )
    load_slope = pltpu.make_async_copy(slope_hbm, slope_ref, sem)
    load_slope.start()
    pos8_ref[...] = jnp.zeros(pos8_ref.shape, F32)
    pos8_ref[0:3, :] = pos_ref[:, 0, :]
    stacked = [part.astype(F32) for part in split3(pos8_ref[...])] + [jnp.zeros((C - 24, ATOMS), F32)]
    stacked = jnp.concatenate(stacked, axis=0).astype(BF16)
    cells, within = neighbour_parts(neigh_ref)
    cells_ref[...] = cells
    within_ref[...] = within
    live_row = jnp.maximum(counts_ref[...].astype(F32) - float(HALF), 0.0)
    square = (ATOMS, ATOMS)
    row_id, col_id = iota(square, 0), iota(square, 1)
    live_col = jnp.sum(jnp.where(row_id == col_id, live_row, 0.0), axis=1, keepdims=True)
    start_col = jnp.sum(jnp.where(col_id < row_id, live_row, 0.0), axis=1, keepdims=True)
    start_row = jnp.sum(jnp.where(row_id < col_id, live_col, 0.0), axis=0, keepdims=True)
    total = jnp.sum(live_row).astype(jnp.int32)
    chunks = (total + GHOST_ROWS - 1) // GHOST_ROWS
    acc_ref[...] = acc_own_ref[...]

    def whole(gathered):
        return gathered + (pltpu.roll(gathered, C - 8, 1) + pltpu.roll(gathered, C - 16, 1))

    def spread_of(start, count):
        place = (iota((ATOMS, count), 1) + start).astype(F32)
        return jnp.logical_and(place >= start_col, place < start_col + live_col)

    def geometry(start, count):
        rows = pl.ds(start, count)
        place = (iota((count, 1), 0) + start).astype(F32)
        inside = jnp.logical_and(place >= start_row, place < start_row + live_row)
        begin = jnp.sum(jnp.where(inside, start_row, 0.0), axis=1, keepdims=True)
        spread = onehot_of(inside)
        named = dot_nt(spread, cells_ref[...]) * 8.0 + dot_nt(spread, within_ref[...])
        named = select_lane(named, (place - begin).astype(jnp.int32) + HALF, 0.0)
        onehot = onehot_of(iota((count, GHOST), 1).astype(F32) == named - float(ATOMS))
        row = named.astype(jnp.int32) - ATOMS
        inside = row >= 0
        row = jnp.maximum(row, 0)
        spots = [(row >> shift) & 3 for shift in (7, 5, 3)]
        moves = [jnp.where(spot == 0, -1, jnp.where(spot == 3, 1, 0)) for spot in spots]
        toward = moves[0] * 9 + moves[1] * 3 + moves[2] + 13
        slot = row & 7
        for at, spot in enumerate(spots):
            slot = slot + (((spot + 1) & 1) << (5 - at))
        place = jnp.where(inside, toward * ATOMS + slot, -1)
        hot_ref[rows, :] = onehot
        gslot_ref[rows, :] = onehot_of(iota((count, TILES * C), 1) == place)
        gatom_ref[rows, :] = spread
        lane = iota((count, C), 1)
        last = dot(onehot, table_ref[:, FEAT - C :])
        image = jnp.zeros((count, C), F32)
        for at, move in enumerate(moves):
            image = jnp.where(lane == at, move.astype(F32) * 4.0, image)
        rel = (whole(last[:, C:]) + image) - whole(dot_nt(spread, stacked))
        rel = jnp.where(jnp.logical_and(lane < 3, inside), rel, 0.0)
        grelt_ref[:, rows] = rel.T[:8]
        last_ref[rows, :] = last[:, :C].astype(BF16)
        radial_of(rel, rbf_ref, radial_ref, rad_ref, drad_ref, rows)

    tails = jnp.maximum(total - HEAD + TAIL - 1, 0) // TAIL
    tail_at = lambda at: pl.multiple_of(HEAD + at * TAIL, TAIL)
    geometry(0, HEAD)

    @pl.loop(0, tails)
    def _(at):
        geometry(tail_at(at), TAIL)

    @pl.loop(0, chunks)
    def _(chunk):
        rows = pl.ds(pl.multiple_of(chunk * GHOST_ROWS, GHOST_ROWS), GHOST_ROWS)

        def put_slope(lanes, value):
            gslope_ref[rows, lanes] = value

        onehot, last = hot_ref[rows, :], last_ref[rows, :]
        gather = onehot_of(spread_of(chunk * GHOST_ROWS, GHOST_ROWS))
        edge_forward(onehot, table_ref, rad_ref, drad_ref, rows, block_ref, mix_ref, lhs_ref, message_ref, put_slope, last)
        for pair in PAIRS:
            lanes = slice(pair[0] * C, (pair[-1] + 1) * C)
            acc_ref[:, lanes] += dot(gather, message_ref[:, lanes])

    for copy in loads:
        copy.wait()
    for pair in PAIRS:
        lanes = slice(pair[0] * C, (pair[-1] + 1) * C)
        low = (acc_ref[:, lanes] * NORM).astype(BF16)
        updated_ref[:, lanes] = dot(low, pair_weight(pair, oblock_ref, out_ref))
    energy = None
    for k in range(COEFFS):
        lanes = slice(k * C, (k + 1) * C)
        value = feat_ref[:, lanes].astype(F32) + updated_ref[:, lanes]
        new_ref[:, lanes] = value.astype(BF16)
        if k == 0:
            logistic = jax.nn.sigmoid(value)
            scale = energy_ref[...]
            term = scale * value * logistic
            grad = scale * logistic * (1.0 + value * (1.0 - logistic))
        else:
            degree = DEGREE[k]
            scaled = norm_ref[degree - 1 : degree, :] * (1.0 / (2 * degree + 1)) * value
            term = scaled * value
            grad = 2.0 * scaled
        energy = term if energy is None else energy + term
        grad_ref[:, lanes] = grad.astype(BF16)
    for pair in PAIRS:
        lanes = slice(pair[0] * C, (pair[-1] + 1) * C)
        weight = pair_weight(pair, oblock_ref, out_ref)
        gsum_ref[lanes, :] = (dot_nt(weight, grad_ref[:, lanes]) * NORM).astype(BF16)
    energy = jnp.sum(energy, axis=1, keepdims=True)
    energies_ref[...] = jnp.sum(jnp.where(row_id == col_id, energy, 0.0), axis=0, keepdims=True)

    def pull_of(relt, slope_grad):
        square = jnp.sum(relt * relt, axis=0, keepdims=True)
        pull = relt * (slope_grad * jnp.where(square > 0.0, lax.rsqrt(square), 0.0))
        high = pull.astype(BF16)
        return jnp.concatenate([high, (pull - high.astype(F32)).astype(BF16)], axis=0)

    load_slope.wait()

    own_total = jnp.zeros((16, ATOMS), F32)
    for start in range(0, ATOMS * HALF, OWN_ROWS):
        rows = slice(start, start + OWN_ROWS)
        slopes = dot(slope_ref[rows, :], gsum_ref[...]).T
        own = (iota((ATOMS, OWN_ROWS), 1) + start) // HALF == iota((ATOMS, OWN_ROWS), 0)
        slopes = jnp.sum(jnp.where(own, slopes, 0.0), axis=0, keepdims=True)
        own_total = own_total + dot(pull_of(relt_ref[:, rows], slopes), pair_ref[rows, :])

    def ghost_step(start, count, totals):
        own_total, ghost_total = totals
        rows = pl.ds(start, count)
        slopes = dot(gslope_ref[rows, :], gsum_ref[...]).T
        slopes = jnp.sum(jnp.where(spread_of(start, count), slopes, 0.0), axis=0, keepdims=True)
        pull = pull_of(grelt_ref[:, rows], slopes)
        return own_total - dot(pull, gatom_ref[rows, :]), ghost_total + dot(pull, gslot_ref[rows, :])

    totals = ghost_step(0, HEAD, (own_total, jnp.zeros((16, TILES * C), F32)))
    own_total, ghost_total = lax.fori_loop(0, tails, lambda at, total: ghost_step(tail_at(at), TAIL, total), totals)
    grad_own_ref[...] = own_total[:8] + own_total[8:]
    for tile in range(TILES):
        lanes = slice(tile * C, (tile + 1) * C)
        tiles_ref[tile] = ghost_total[:8, lanes] + ghost_total[8:, lanes]


def ghost_edges(*operands):
    vmem = pl.BlockSpec(memory_space=pltpu.VMEM)
    hbm = pl.BlockSpec(memory_space=pl.ANY)
    own = ATOMS * HALF
    return pl.pallas_call(
        ghost_body,
        out_shape=(
            jax.ShapeDtypeStruct((ATOMS, FEAT), BF16),
            jax.ShapeDtypeStruct((1, ATOMS), F32),
            jax.ShapeDtypeStruct((8, ATOMS), F32),
            jax.ShapeDtypeStruct((TILES, 8, C), F32),
        ),
        in_specs=[pl.BlockSpec(memory_space=pltpu.HBM)] * 2 + [vmem] * 14 + [hbm],
        out_specs=(vmem,) * 4,
        scratch_shapes=like(operands[:2])
        + [
            pltpu.VMEM((8, ATOMS), F32),
            pltpu.VMEM((SLOTS, ATOMS), BF16),
            pltpu.VMEM((SLOTS, ATOMS), BF16),
            pltpu.VMEM((GHOST_EDGES, DEGREES * C), BF16),
            pltpu.VMEM((GHOST_EDGES, DEGREES * C), BF16),
            pltpu.VMEM((2 * GHOST_ROWS, FEAT), BF16),
            pltpu.VMEM((GHOST_ROWS, FEAT), BF16),
            pltpu.VMEM((own, FEAT), BF16),
            pltpu.VMEM((GHOST_EDGES, FEAT), BF16),
            pltpu.VMEM((ATOMS, FEAT), F32),
            pltpu.VMEM((8, GHOST_EDGES), F32),
            pltpu.VMEM((GHOST_EDGES, TILES * C), BF16),
            pltpu.VMEM((GHOST_EDGES, ATOMS), BF16),
            pltpu.VMEM((GHOST_EDGES, GHOST), BF16),
            pltpu.VMEM((GHOST_EDGES, C), BF16),
            pltpu.VMEM((ATOMS, FEAT), F32),
            pltpu.VMEM((ATOMS, FEAT), BF16),
            pltpu.VMEM((FEAT, ATOMS), BF16),
            pltpu.SemaphoreType.DMA,
        ],
        compiler_params=pltpu.CompilerParams(vmem_limit_bytes=VMEM_LIMIT),
        cost_estimate=pl.CostEstimate(flops=10_000_000_000, bytes_accessed=14_000_000, transcendentals=400_000),
        name="ghost_edges",
    )(*operands)


def return_body(tiles_ref, grad_own_ref, order_hbm, forces_ref, order_ref, load_sem, landed_ref, send_sem, recv_sem):
    loads = load_all((order_hbm,), (order_ref,), load_sem)
    here = [lax.axis_index(axis) for axis in ("gx", "gy", "gz")]
    sizes = [lax.axis_size(axis) for axis in ("gx", "gy", "gz")]
    barrier = pltpu.get_barrier_semaphore()
    others = [at for at in range(DIRECTIONS) if at != DIRECTIONS // 2]
    copies = []
    for at in others:
        moves = (at // 9 - 1, at // 3 % 3 - 1, at % 3 - 1)
        device = tuple(lax.rem(h + n + m, n) for h, n, m in zip(here, sizes, moves))
        pl.semaphore_signal(barrier, inc=1, device_id=device, device_id_type=MESH_ID)
        copies.append(
            pltpu.make_async_remote_copy(
                src_ref=tiles_ref.at[at // 2], dst_ref=landed_ref.at[at],
                send_sem=send_sem.at[at], recv_sem=recv_sem.at[at],
                device_id=device, device_id_type=MESH_ID,
            )
        )
    pl.semaphore_wait(barrier, len(others))
    for copy in copies:
        copy.start()
    loads[0].wait()
    listed = column_of(order_ref[...].astype(F32)) == iota((ATOMS, ATOMS), 1).astype(F32)
    listed = onehot_of(listed)
    for copy in copies:
        copy.wait_recv()
    even = sum(landed_ref[at] for at in others if at % 2 == 0)
    odd = sum(landed_ref[at] for at in others if at % 2 == 1)
    total = (even + pltpu.roll(odd, ATOMS, 1))[:, :ATOMS]
    back = sum(dot(part, listed) for part in split3(total)[::-1])
    forces_ref[:, 0, :] = -(grad_own_ref[...] + back)[:3]
    for copy in copies:
        copy.wait_send()


def return_forces(tiles, grad_own, order):
    vmem = pl.BlockSpec(memory_space=pltpu.VMEM)
    return pl.pallas_call(
        return_body,
        out_shape=jax.ShapeDtypeStruct((3, 1, ATOMS), F32),
        in_specs=[vmem] * 2 + [pl.BlockSpec(memory_space=pltpu.HBM)],
        out_specs=vmem,
        scratch_shapes=like((order,))
        + [
            pltpu.VMEM((DIRECTIONS, 8, C), F32),
            pltpu.SemaphoreType.DMA((DIRECTIONS,)),
            pltpu.SemaphoreType.DMA((DIRECTIONS,)),
        ],
        compiler_params=pltpu.CompilerParams(collective_id=1, has_side_effects=True, vmem_limit_bytes=4 * 1024 * 1024),
        name="return_forces",
    )(tiles, grad_own, order)


def local(
    features, positions, neighbours, counts, cell_atoms,
    rbf_weight, radial_weight, mix_weight, out_weight, energy_weight, norm_weight,
):
    feat = features.reshape(ATOMS, FEAT)
    pos = positions.reshape(3, 1, ATOMS)
    neigh = jnp.transpose(neighbours.reshape(ATOMS, SLOTS))
    live = counts.reshape(1, ATOMS)
    order = cell_atoms.reshape(1, ATOMS)
    energy, norm = energy_weight.reshape(1, C), norm_weight
    feat, pos, neigh, live, order, rbf_weight, radial_weight, mix_weight, out_weight, energy, norm = (
        pltpu.with_memory_space_constraint(operand, pltpu.HBM)
        for operand in (feat, pos, neigh, live, order, rbf_weight, radial_weight, mix_weight, out_weight, energy, norm)
    )
    held = own_edges(
        feat, pos, neigh, live, order, rbf_weight, radial_weight, mix_weight, out_weight
    )
    acc, relt, pairs, table, blocks, oblocks, slopes = held[9:]
    updated, energies, grad_own, tiles = ghost_edges(
        energy, norm, *held[:4], *held[5:9], acc, relt, pairs, table.reshape(GHOST, WIDE), blocks, oblocks, slopes
    )
    forces = return_forces(tiles, grad_own, order)
    return (
        updated.reshape(features.shape),
        energies.reshape(counts.shape),
        forces.reshape(positions.shape),
    )


def solution(mesh):
    spread = P("gx", "gy", "gz", None, None)
    rows = P("gx", "gy", "gz", None)
    return jax.shard_map(
        local,
        mesh=mesh,
        in_specs=(spread, spread, spread, rows, rows) + (P(),) * 6,
        out_specs=(spread, rows, spread),
        check_vma=False,
    )
```
